256 devices in a mesh: arc: 2 (over core), row: 8 (over x, z_hi), col: 16 (over y, z_lo).
Axes of the slice: x: 4, y: 4, z: 8 (z_hi: 2, z_lo: 4; z = z_hi * 4 + z_lo), core: 2. Of those that a mesh axis runs over, the one named last changes fastest.
Arguments:
- design: bfloat16 [24576, 6, 16, 64], P(('arc', 'row'), None, 'col'), may hold values from -0.03827328 to 0.03827328
- obs_weight: float32 [24576], P(('arc', 'row')), may hold values from 0.25 to 4
- prior: float32 [6, 16, 64], P(None, 'col'), may hold values from 0.3 to 3
Outputs:
- normal: float32 [12, 8, 64, 6, 16, 64], P(None, 'row', None, None, 'col')
- panel: float32 [12, 8, 64, 1024], P(None, 'row')
The draws below stay inside these ranges and needn't reach their ends.
All inputs are finite; a program needn't handle non-finite values.
Results may differ from the reference program's by a relative error of at most 0.0012.
Values may be sent and summed in bfloat16 or wider, within the bound.
A program may use at most 128 MiB of HBM per device.

```python
import math
import jax
import jax.numpy as jnp
from jax import lax

K = 6144
PW = 1024
ROWS = 24576
TB = 64
KC = 6
KT_R = 12
N_ROW = 8
N_COL = 16


def draw_design(key, part):
    key = jax.random.fold_in(key, 11)
    noise_key, common_key, loading_key = jax.random.split(key, 3)
    group_width = 64
    groups = K // group_width
    factor = 0.8 * float(ROWS) ** (-0.5)
    noise = jnp.clip(jax.random.normal(noise_key, (ROWS, groups, group_width), jnp.float32), -4.0, 4.0)
    common = jnp.clip(jax.random.normal(common_key, (ROWS, groups, 1), jnp.float32), -3.0, 3.0)
    loading = jax.random.uniform(loading_key, (1, groups, group_width), jnp.float32, 0.4, 0.8)
    values = (noise + loading * common) * factor
    return values.reshape(ROWS, KC, N_COL, TB).astype(jnp.bfloat16)


def level_of(key, dims, cuts, least, largest):
    def one(position, shards_of):
        draws = jax.random.uniform(jax.random.fold_in(jax.random.fold_in(key, 6), position), (shards_of,), jnp.float32, least / len(cuts), largest / len(cuts))
        return jnp.repeat(jnp.exp(draws), dims[position] // shards_of).reshape((-1,) + (1,) * (len(dims) - position - 1))

    gain = one(*cuts[0])
    for cut in cuts[1:]:
        gain = gain * one(*cut)
    return gain


def setup_inputs(seed: int = 0) -> dict:
    key_of = jax.random.split(jax.random.key(seed), 4)
    design = draw_design(jax.random.fold_in(key_of[3], 71), 0)
    obs_weight = jnp.clip(jnp.exp(math.log(4.0) - 2.7725887 * jax.random.uniform(key_of[1], (ROWS,), jnp.float32) ** level_of(key_of[1], (ROWS,), ((0, 16),), -0.2, 0.2)), 0.25, 4.0)
    prior = jnp.clip(jnp.exp(math.log(3.0) - 2.3025851 * jax.random.uniform(key_of[2], (KC, N_COL, TB), jnp.float32) ** level_of(key_of[2], (KC, N_COL, TB), ((1, 16),), -0.2, 0.2)), 0.3, 3.0)
    return dict(design=design, obs_weight=obs_weight, prior=prior)


def reference(design, obs_weight, prior):
    rows = design.shape[0]
    flat = design.reshape(rows, K)
    weighted = (flat.astype(jnp.float32) * obs_weight[:, None]).astype(jnp.bfloat16)
    gram = jnp.dot(flat.astype(jnp.float32).T.astype(jnp.float32), weighted.astype(jnp.float32), precision=lax.Precision.HIGHEST, preferred_element_type=jnp.float32)
    gram = gram + jnp.diag(prior.reshape(K))
    normal = gram.reshape(KT_R, N_ROW, TB, KC, N_COL, TB)
    factor = jnp.linalg.cholesky(gram[:PW, :PW])
    panel = lax.linalg.triangular_solve(factor, gram[:, :PW], left_side=False, lower=True, transpose_a=True)
    return (normal, panel.reshape(KT_R, N_ROW, TB, PW))
```

```python
import functools

import jax
import jax.numpy as jnp
from jax import lax
from jax.experimental import pallas as pl
from jax.experimental.pallas import tpu as pltpu
from jax.sharding import PartitionSpec as P

F32 = jnp.float32
BF16 = jnp.bfloat16
MESH = pl.DeviceIdType.MESH
VMEM = pl.BlockSpec(memory_space=pltpu.VMEM)
HIGHEST = lax.Precision.HIGHEST


def place():
    arc = lax.axis_index("arc")
    row = lax.axis_index("row")
    col = lax.axis_index("col")
    return arc, row // 2, row % 2, col // 4, col % 4


def device(arc, x, zh, y, zl):
    return (arc, x * 2 + zh, y * 4 + zl)


def host(z1, z2):
    low, high = jnp.minimum(z1, z2), jnp.maximum(z1, z2)
    apart = jnp.where(high == 2, 2, jnp.where(high == 1, 0, jnp.where(low == 2, 3, low)))
    return jnp.where(z1 == z2, z1, apart)


def pick(values, at):
    out = jnp.int32(values[0])
    for k in range(1, len(values)):
        out = jnp.where(at == k, values[k], out)
    return out


def gram_kernel(at_ref, w_ref, out_ref, ya, za, yw, zw, part, dbuf, xbuf, total, fbuf,
                ysend, yrecv, zsend, zrecv, dsend, drecv, xsend, xrecv, fsend, frecv, osend, orecv):
    arc, x, zh, y, zl = place()
    size, obs = at_ref.shape
    half, piece = size // 2, size // 8
    even = zl % 2 == 0
    moved = (pick((1, 3, 0, 2), zl), pick((3, 0, 1, 0), zl))
    goes = (pick((2, 0, 3, 1), zl), pick((0, 2, 0, 0), zl))
    mate = device(1 - arc, x, zh, y, zl)

    def owner(block):
        kind, slot, k = block
        other = (y + k) % 4
        if kind == "own":
            y1, z1, y2, z2 = y, zl, other, zl
        elif kind == "rows":
            y1, z1, y2, z2 = y, moved[slot], other, zl
        else:
            y1, z1, y2, z2 = other, zl, y, moved[slot]
        r = (y1 % 2) * 4 + z1
        target = (arc, r, y2 * 4 + z2)
        own_r = x * 2 + zh
        mine = (r == own_r) & (y2 == y) & (z2 == zl)
        return target, y1 // 2, mine

    blocks = [("own", 0, k) for k in range(4)]
    for slot in range(2):
        blocks += [("rows", slot, k) for k in range(4)] + [("cols", slot, k) for k in range(4)]

    bar = pltpu.get_barrier_semaphore()

    def greet(target):
        pl.semaphore_signal(bar, inc=1, device_id=target, device_id_type=MESH)

    count = jnp.int32(3 + 3 + 1 + 1)
    for k in (1, 2, 3):
        greet(device(arc, x, zh, (y + k) % 4, zl))
        greet(device(arc, (x + k) % 4, zh, y, zl))
    greet(mate)
    greet(device(arc, x, zh, y, moved[0]))

    @pl.when(even)
    def _():
        greet(device(arc, x, zh, y, moved[1]))

    count = count + jnp.where(even, 0, 1)
    r_own = x * 2 + zh
    for upper in range(2):
        y1, z1 = r_own // 4 + 2 * upper, r_own % 4
        plane = host(z1, zl)
        yy = jnp.where(z1 == zl, y1, jnp.where(plane == zl, y1, y))
        for xx in range(4):
            for zz in range(2):
                same = (xx == x) & (zz == zh) & (yy == y) & (plane == zl)

                @pl.when(jnp.logical_not(same))
                def _():
                    greet(device(arc, xx, zz, yy, plane))

    for b, block in enumerate(blocks):
        away = jnp.where(owner(block)[2], 0, 1)
        count = count + (away if b < 12 else jnp.where(even, away, 0))
    pl.semaphore_wait(bar, count)

    ycopies = []
    for k in (1, 3, 2):
        c = pltpu.make_async_remote_copy(at_ref, ya.at[(4 - k) % 4], ysend.at[k], yrecv.at[(4 - k) % 4],
                                         device_id=device(arc, x, zh, (y + k) % 4, zl), device_id_type=MESH)
        ycopies.append(c)
    zcopies = [pltpu.make_async_remote_copy(at_ref, za.at[s], zsend.at[s], zrecv.at[s],
                                            device_id=device(arc, x, zh, y, goes[s]), device_id_type=MESH)
               for s in range(2)]
    zcopies[0].start()

    @pl.when(jnp.logical_not(even))
    def _():
        zcopies[1].start()

    for c in ycopies:
        c.start()

    weight = w_ref[...]

    def weigh(src, dst):
        def chunk(i, carry):
            at = pl.ds(pl.multiple_of(i * 32, 32), 32)
            dst[at, :] = (src[at, :].astype(F32) * weight).astype(BF16)
            return carry

        lax.fori_loop(0, size // 32, chunk, 0)

    def times(left, right, into):
        into[...] = lax.dot_general(left[...], right[...], (((1,), (1,)), ((), ())), preferred_element_type=F32)

    def trade(first, n):
        return pltpu.make_async_remote_copy(
            part.at[pl.ds(first, n), pl.ds(pl.multiple_of((1 - arc) * half, half), half)],
            dbuf.at[pl.ds(first, n)], dsend.at[first // 4], drecv.at[first // 4],
            device_id=mate, device_id_type=MESH)

    def spread(first, n, k):
        peer = (x + k) % 4
        return pltpu.make_async_remote_copy(
            part.at[pl.ds(first, n), pl.ds(pl.multiple_of(arc * half + peer * piece, 16), piece)],
            xbuf.at[(4 - k) % 4, pl.ds(first, n)], xsend.at[k, first // 4], xrecv.at[(4 - k) % 4, first // 4],
            device_id=device(arc, peer, zh, y, zl), device_id_type=MESH)

    def halves(first, n):
        trade(first, n).wait()
        rows = pl.ds(pl.multiple_of(arc * half, half), half)

        def add(b, carry):
            part[first + b, rows] = part[first + b, rows] + dbuf[first + b]
            return carry

        lax.fori_loop(0, n, add, 0)
        for k in (1, 3, 2):
            spread(first, n, k).start()

    def deliver(first, n):
        for k in (1, 3, 2):
            spread(first, n, k).wait()
        rows = pl.ds(pl.multiple_of(arc * half + x * piece, 16), piece)

        def add(b, carry):
            at = first + b
            total[at] = (part[at, rows] + xbuf[1, at]) + (xbuf[2, at] + xbuf[3, at])
            return carry

        lax.fori_loop(0, n, add, 0)
        for b in range(first, first + n):
            final(b, "start")

    def final(b, act):
        target, upper, mine = owner(blocks[b])
        dst = fbuf.at[upper, zh, x]
        sem = frecv.at[upper, zh, x]

        @pl.when(mine)
        def _():
            if act == "start":
                pltpu.make_async_copy(total.at[b], dst, sem).start()

        @pl.when(jnp.logical_not(mine))
        def _():
            c = pltpu.make_async_remote_copy(total.at[b], dst, fsend.at[b], sem, device_id=target, device_id_type=MESH)
            if act == "start":
                c.start()
            else:
                c.wait_send()

    ya[0] = at_ref[...]
    weigh(at_ref, yw.at[0])
    for k in (1, 3, 2):
        pltpu.make_async_remote_copy(at_ref, ya.at[k], ysend.at[k], yrecv.at[k], device_id=mate, device_id_type=MESH).wait_recv()
        weigh(ya.at[k], yw.at[k])

    def own_block(k, carry):
        times(at_ref, yw.at[k], part.at[k])
        return carry

    lax.fori_loop(0, 4, own_block, 0)
    trade(0, 4).start()

    def moved_blocks(s):
        zcopies[s].wait_recv()
        weigh(za.at[s], zw.at[s])

        def one(k, carry):
            times(za.at[s], yw.at[k], part.at[4 + 8 * s + k])
            times(ya.at[k], zw.at[s], part.at[8 + 8 * s + k])
            return carry

        lax.fori_loop(0, 4, one, 0)
        trade(4 + 8 * s, 8).start()

    moved_blocks(0)
    halves(0, 4)

    @pl.when(even)
    def _():
        moved_blocks(1)

    halves(4, 8)

    @pl.when(even)
    def _():
        halves(12, 8)

    deliver(0, 4)
    deliver(4, 8)

    @pl.when(even)
    def _():
        deliver(12, 8)

    for upper in range(2):
        for xx in range(4):
            for zz in range(2):
                pltpu.make_async_copy(total.at[0], fbuf.at[upper, zz, xx], frecv.at[upper, zz, xx]).wait()
            at = pl.ds(pl.multiple_of(arc * half + xx * piece, 16), piece)
            out_ref[upper, at] = fbuf[upper, 0, xx] + fbuf[upper, 1, xx]
    rows = pl.ds(pl.multiple_of(arc * half, half), half)
    back = pltpu.make_async_remote_copy(out_ref.at[:, rows], out_ref.at[:, rows], osend, orecv,
                                        device_id=mate, device_id_type=MESH)
    back.start()

    for c in ycopies:
        c.wait_send()
    zcopies[0].wait_send()

    @pl.when(jnp.logical_not(even))
    def _():
        zcopies[1].wait_send()

    for b in range(12):
        final(b, "end")

    @pl.when(even)
    def _():
        for b in range(12, 20):
            final(b, "end")

    back.wait()


def gram_block(at, weight):
    size, obs = at.shape
    dma = pltpu.SemaphoreType.DMA
    return pl.pallas_call(
        gram_kernel,
        out_shape=jax.ShapeDtypeStruct((2, size, size), F32),
        in_specs=[VMEM, VMEM],
        out_specs=VMEM,
        scratch_shapes=[
            pltpu.VMEM((4, size, obs), BF16),
            pltpu.VMEM((2, size, obs), BF16),
            pltpu.VMEM((4, size, obs), BF16),
            pltpu.VMEM((2, size, obs), BF16),
            pltpu.VMEM((20, size, size), F32),
            pltpu.VMEM((20, size // 2, size), F32),
            pltpu.VMEM((4, 20, size // 8, size), F32),
            pltpu.VMEM((20, size // 8, size), F32),
            pltpu.VMEM((2, 2, 4, size // 8, size), F32),
            dma((4,)), dma((4,)), dma((2,)), dma((2,)), dma((5,)), dma((5,)),
            dma((4, 5)), dma((4, 5)), dma((20,)), dma((2, 2, 4)), dma, dma,
        ],
        compiler_params=pltpu.CompilerParams(collective_id=0, has_side_effects=True, vmem_limit_bytes=58 << 20),
        name="gram_block",
    )(at, weight)


def factor_inverse(block):
    n = block.shape[0]
    lane = lax.broadcasted_iota(jnp.int32, (8, n), 1)
    sub = lax.broadcasted_iota(jnp.int32, (8, n), 0)
    groups = [block[8 * g : 8 * g + 8, :] for g in range(n // 8)]
    for q in range(n // 8):
        pivot = groups[q]
        inside = (lane >= 8 * q) & (lane < 8 * q + 8)
        cols = [jnp.broadcast_to(pivot[:, 8 * q + j : 8 * q + j + 1], (8, n)) for j in range(8)]
        rows = jnp.where(inside, (lane - 8 * q == sub).astype(F32), pivot)
        scale, mult, scaled = [], {}, []
        for j in range(8):
            r = lax.rsqrt(cols[j][j : j + 1, :])
            scale.append(r)
            m = jnp.where(sub > j, cols[j] * r, 0.0)
            for l in range(j + 1, 8):
                mult[j, l] = cols[l][j : j + 1, :] * r
                cols[l] = cols[l] - m * mult[j, l]
            top = rows[j : j + 1, :] * r
            scaled.append(top)
            rows = jnp.where(sub == j, top, rows - m * top)
        groups[q] = rows
        for g in range(q + 1, n // 8):
            low = groups[g]
            c = [jnp.broadcast_to(low[:, 8 * q + j : 8 * q + j + 1], (8, n)) for j in range(8)]
            low = jnp.where(inside, 0.0, low)
            for j in range(8):
                m = c[j] * scale[j]
                for l in range(j + 1, 8):
                    c[l] = c[l] - m * mult[j, l]
                low = low - m * scaled[j]
            groups[g] = low
    lane_all = lax.broadcasted_iota(jnp.int32, (n, n), 1)
    sub_all = lax.broadcasted_iota(jnp.int32, (n, n), 0)
    return jnp.where(lane_all <= sub_all, jnp.concatenate(groups, axis=0), 0.0)


def inverse_factor(v_ref):
    n, b = v_ref.shape[0], 128
    steps = n // b

    def step(p, carry):
        at = pl.ds(pl.multiple_of(p * b, b), b)
        inv = factor_inverse(v_ref[at, at])
        v_ref[at, at] = jnp.eye(b, dtype=F32)
        v_ref[at, :] = jnp.dot(inv, v_ref[at, :], precision=HIGHEST, preferred_element_type=F32)

        def below(i, carry):
            here = pl.ds(pl.multiple_of(i * b, b), b)
            left = v_ref[at, here]
            v_ref[here, at] = jnp.zeros((b, b), F32)
            v_ref[here, :] = v_ref[here, :] - lax.dot_general(
                left, v_ref[at, :], (((0,), (0,)), ((), ())), precision=HIGHEST, preferred_element_type=F32)
            return carry

        lax.fori_loop(p + 1, steps, below, 0)
        return carry

    lax.fori_loop(0, steps, step, 0)


def panel_kernel(lead_ref, out_ref, gt, g11, v, zs, zr, ys, yr, cs, cr, hs, hr, xs, xr, ms, mr):
    arc, x, zh, y, zl = place()
    col = y * 4 + zl
    row = x * 2 + zh
    mate = device(1 - arc, x, zh, y, zl)
    bar = pltpu.get_barrier_semaphore()

    def greet(target):
        pl.semaphore_signal(bar, inc=1, device_id=target, device_id_type=MESH)

    greet(mate)
    greet(device(arc, x, 1 - zh, y, zl))
    for k in (1, 2, 3):
        greet(device(arc, x, zh, y, (zl + k) % 4))
        greet(device(arc, x, zh, (y + k) % 4, zl))
        greet(device(arc, (x + k) % 4, zh, y, zl))
    pl.semaphore_wait(bar, 11)

    parts = (pl.ds(0, 128), pl.ds(128, 640))

    def along_z(p, k):
        to = (zl + k) % 4
        return pltpu.make_async_remote_copy(
            lead_ref.at[arc, :, parts[p]], gt.at[col, arc, :, parts[p]], zs.at[p, k], zr.at[p, (4 - k) % 4],
            device_id=device(arc, x, zh, y, to), device_id_type=MESH)

    def along_y(p, k):
        view = gt.at[pl.ds(y * 4, 4), arc, :, parts[p]]
        return pltpu.make_async_remote_copy(
            view, view, ys.at[p, k], yr.at[p, (4 - k) % 4],
            device_id=device(arc, x, zh, (y + k) % 4, zl), device_id_type=MESH)

    def across(p):
        view = gt.at[:, arc, :, parts[p]]
        return pltpu.make_async_remote_copy(view, view, cs.at[p], cr.at[p], device_id=mate, device_id_type=MESH)

    for p in range(2):
        for k in (1, 3, 2):
            along_z(p, k).start()
    gt[col, arc] = lead_ref[arc]
    for p in range(2):
        for k in (1, 3, 2):
            along_z(p, k).wait()
        for k in (1, 3, 2):
            along_y(p, k).start()
        if p == 0:
            for k in (1, 3, 2):
                along_y(p, k).wait()
            for c in range(16):
                g11[row, c, arc] = gt[c, arc, :, 0:128]
            view = g11.at[row, :, arc]
            hop = pltpu.make_async_remote_copy(view, view, hs, hr, device_id=device(arc, x, 1 - zh, y, zl), device_id_type=MESH)
            hop.start()
            hop.wait()
            view = g11.at[pl.ds(x * 2, 2), :, arc]
            hops = [pltpu.make_async_remote_copy(view, view, xs.at[k], xr.at[(4 - k) % 4],
                                                 device_id=device(arc, (x + k) % 4, zh, y, zl), device_id_type=MESH)
                    for k in (1, 3, 2)]
            for h in hops:
                h.start()
            for h in hops:
                h.wait()
            view = g11.at[:, :, arc]
            hop = pltpu.make_async_remote_copy(view, view, ms, mr, device_id=mate, device_id_type=MESH)
            hop.start()
            hop.wait()
            across(0).start()

    def assemble(c, carry):
        at = pl.ds(pl.multiple_of(c * 64, 64), 64)
        for j in range(8):
            lanes = pl.ds((j // 4) * 64, 64)
            first, second = 2 * (j % 4), 2 * (j % 4) + 1
            v[at, j * 128 : j * 128 + 128] = jnp.concatenate(
                [g11[first, c].reshape(64, 128)[:, (j // 4) * 64 : (j // 4) * 64 + 64],
                 g11[second, c].reshape(64, 128)[:, (j // 4) * 64 : (j // 4) * 64 + 64]], axis=1)
        return carry

    lax.fori_loop(0, 16, assemble, 0)

    def symmetric(i, carry):
        at = pl.ds(pl.multiple_of(i * 128, 128), 128)

        def one(j, carry):
            here = pl.ds(pl.multiple_of(j * 128, 128), 128)
            upper = v[at, here]
            mean = 0.5 * (upper + v[here, at].T)
            v[at, here] = mean
            v[here, at] = mean.T
            return carry

        return lax.fori_loop(i, 8, one, carry)

    lax.fori_loop(0, 8, symmetric, 0)
    inverse_factor(v)
    for j in range(4):
        v[j * 256 : j * 256 + 128, j * 256 + 128 : j * 256 + 256] = jnp.zeros((128, 128), F32)

    for k in (1, 3, 2):
        along_y(1, k).wait()
    across(1).start()
    for p in range(2):
        across(p).wait()

    def strip(j, carry):
        at = pl.ds(pl.multiple_of(j * 256, 256), 256)

        def one(k, total):
            here = pl.ds(pl.multiple_of(k * 256, 256), 256)
            rows = gt[pl.ds(k * 4, 4)].reshape(256, 768)
            return total + jnp.dot(v[at, here], rows, precision=HIGHEST, preferred_element_type=F32)

        total = lax.fori_loop(0, j + 1, one, jnp.zeros((256, 768), F32))
        out_ref[:, at] = total.T
        return carry

    lax.fori_loop(0, 4, strip, 0)


def panel_rows(lead):
    dma = pltpu.SemaphoreType.DMA
    width = lead.shape[-1]
    return pl.pallas_call(
        panel_kernel,
        out_shape=jax.ShapeDtypeStruct((width, 1024), F32),
        in_specs=[VMEM],
        out_specs=VMEM,
        scratch_shapes=[
            pltpu.VMEM((16, 2, 32, width), F32),
            pltpu.VMEM((8, 16, 2, 32, 128), F32),
            pltpu.VMEM((1024, 1024), F32),
            dma((2, 4)), dma((2, 4)), dma((2, 4)), dma((2, 4)), dma((2,)), dma((2,)), dma, dma, dma((4,)), dma((4,)), dma, dma,
        ],
        compiler_params=pltpu.CompilerParams(collective_id=1, has_side_effects=True, vmem_limit_bytes=58 << 20),
        name="panel_rows",
    )(lead)


def body(design, obs_weight, prior):
    rows_dev, kc_tiles, single, tile = design.shape
    n_row, n_col = lax.axis_size("row"), lax.axis_size("col")
    local_cols = kc_tiles * tile
    gram = gram_block(design.transpose(1, 2, 3, 0).reshape(local_cols, rows_dev), obs_weight.reshape(1, rows_dev))
    tiles = gram.reshape(2, kc_tiles, tile, kc_tiles, tile).transpose(1, 0, 2, 3, 4).reshape(2 * kc_tiles, tile, kc_tiles, tile)
    row_id = lax.axis_index("row")
    col_id = lax.axis_index("col")
    kt_rows = 2 * kc_tiles
    tile_rows = jnp.arange(kt_rows, dtype=jnp.int32) * n_row + row_id
    tile_cols = jnp.arange(kc_tiles, dtype=jnp.int32) * n_col + col_id
    same = (tile_rows[:, None] == tile_cols[None, :]).astype(F32)
    added = (same[:, None, :, None] * jnp.eye(tile, dtype=F32)[None, :, None, :]
             * prior.reshape(kc_tiles, tile)[None, None, :, :])
    normal = tiles + added
    lead = normal[:, :, 0, :].reshape(kt_rows * tile, tile).T.reshape(2, tile // 2, kt_rows * tile)
    panel = panel_rows(lead)
    return (normal.reshape(kt_rows, 1, tile, kc_tiles, 1, tile), panel.reshape(kt_rows, 1, tile, 1024))


def solution(mesh):
    placed = (P(("arc", "row"), None, "col", None), P(("arc", "row")), P(None, "col", None))
    return jax.shard_map(
        body,
        mesh=mesh,
        in_specs=placed,
        out_specs=(P(None, "row", None, None, "col", None), P(None, "row", None, None)),
        check_vma=False,
    )
```

```python
import functools

import jax
import jax.numpy as jnp
from jax import lax
from jax.experimental import pallas as pl
from jax.experimental.pallas import tpu as pltpu
from jax.sharding import PartitionSpec as P

F32 = jnp.float32
BF16 = jnp.bfloat16
MESH = pl.DeviceIdType.MESH
VMEM = pl.BlockSpec(memory_space=pltpu.VMEM)
HIGHEST = lax.Precision.HIGHEST


def place():
    arc = lax.axis_index("arc")
    row = lax.axis_index("row")
    col = lax.axis_index("col")
    return arc, row // 2, row % 2, col // 4, col % 4


def device(arc, x, zh, y, zl):
    return (arc, x * 2 + zh, y * 4 + zl)


def pick(values, at):
    out = jnp.int32(values[0])
    for k in range(1, len(values)):
        out = jnp.where(at == k, values[k], out)
    return out


def factor_inverse(block):
    n = block.shape[0]
    lane = lax.broadcasted_iota(jnp.int32, (8, n), 1)
    sub = lax.broadcasted_iota(jnp.int32, (8, n), 0)
    groups = [block[8 * g : 8 * g + 8, :] for g in range(n // 8)]
    for q in range(n // 8):
        pivot = groups[q]
        inside = (lane >= 8 * q) & (lane < 8 * q + 8)
        cols = [jnp.broadcast_to(pivot[:, 8 * q + j : 8 * q + j + 1], (8, n)) for j in range(8)]
        rows = jnp.where(inside, (lane - 8 * q == sub).astype(F32), pivot)
        scale, mult, scaled = [], {}, []
        for j in range(8):
            r = lax.rsqrt(cols[j][j : j + 1, :])
            scale.append(r)
            m = jnp.where(sub > j, cols[j] * r, 0.0)
            for l in range(j + 1, 8):
                mult[j, l] = cols[l][j : j + 1, :] * r
                cols[l] = cols[l] - m * mult[j, l]
            top = rows[j : j + 1, :] * r
            scaled.append(top)
            rows = jnp.where(sub == j, top, rows - m * top)
        groups[q] = rows
        for g in range(q + 1, n // 8):
            low = groups[g]
            c = [jnp.broadcast_to(low[:, 8 * q + j : 8 * q + j + 1], (8, n)) for j in range(8)]
            low = jnp.where(inside, 0.0, low)
            for j in range(8):
                m = c[j] * scale[j]
                for l in range(j + 1, 8):
                    c[l] = c[l] - m * mult[j, l]
                low = low - m * scaled[j]
            groups[g] = low
    lane_all = lax.broadcasted_iota(jnp.int32, (n, n), 1)
    sub_all = lax.broadcasted_iota(jnp.int32, (n, n), 0)
    return jnp.where(lane_all <= sub_all, jnp.concatenate(groups, axis=0), 0.0)


CHUNKS = ((0, 64), (64, 160), (224, 160))
GROUPS = ((0, 9), (9, 3), (12, 8))


def kernel(at_ref, w_ref, prior_ref, norm_ref, panel_ref, out_ref,
           ya, za, yw, zw, part, dbuf, narrow, xf, xb, fbuf, strip, sbuf, mine, sx, sz, seen, v, rcat, gt,
           ysend, yrecv, zsend, zrecv, dsend, drecv, fxs, fxr, bxs, bxr, fsend, frecv, osend, orecv,
           s1s, s1r, s2s, s2r, s3s, s3r, s4s, s4r, s5s, s5r, s6s, s6r, s7s, s7r, gzs, gzr, gys, gyr, gcs, gcr):
    arc, x, zh, y, zl = place()
    size, obs = at_ref.shape
    half, piece = size // 2, size // 8
    even = zl % 2 == 0
    odd = jnp.logical_not(even)
    moved = (pick((1, 3, 0, 2), zl), pick((3, 0, 1, 0), zl))
    goes = (pick((2, 0, 3, 1), zl), pick((0, 2, 0, 0), zl))
    mate = device(1 - arc, x, zh, y, zl)
    zpeer = device(arc, x, 1 - zh, y, zl)
    col, row = y * 4 + zl, x * 2 + zh
    turns = (1, 3, 2)

    def xpeer(k):
        return device(arc, (x + k) % 4, zh, y, zl)

    def ypeer(k):
        return device(arc, x, zh, (y + k) % 4, zl)

    def lpeer(k):
        return device(arc, x, zh, y, (zl + k) % 4)

    def back(at, k):
        return (at + 4 - k) % 4

    def remote(src, dst, send, recv, target):
        return pltpu.make_async_remote_copy(src, dst, send, recv, device_id=target, device_id_type=MESH)

    blocks = [(kind, 0, k) for kind in ("own", "rows", "cols") for k in (0, 1, 3)]
    blocks += [(kind, 0, 2) for kind in ("own", "rows", "cols")]
    blocks += [(kind, 1, k) for kind in ("rows", "cols") for k in range(4)]

    def owner(block):
        kind, slot, k = block
        k = (y + k) % 4
        if kind == "own":
            y1, z1, y2, z2 = y, zl, k, zl
        elif kind == "rows":
            y1, z1, y2, z2 = y, moved[slot], k, zl
        else:
            y1, z1, y2, z2 = k, zl, y, moved[slot]
        r = (y1 % 2) * 4 + z1
        here = (r == row) & (y2 == y) & (z2 == zl)
        return (arc, r, y2 * 4 + z2), y1 // 2, here

    bar = pltpu.get_barrier_semaphore()

    def greet(target):
        pl.semaphore_signal(bar, inc=1, device_id=target, device_id_type=MESH)

    for k in turns:
        greet(ypeer(k))
        greet(xpeer(k))
        greet(lpeer(k))
    greet(mate)
    greet(zpeer)
    pl.semaphore_wait(bar, 11)

    def ycopy(c, k):
        at = pl.ds(*CHUNKS[c])
        return remote(at_ref.at[at], ya.at[y, at], ysend.at[c, k], yrecv.at[c, k], ypeer(k))

    def yarrival(c, k):
        at = pl.ds(*CHUNKS[c])
        return remote(at_ref.at[at], ya.at[back(y, k), at], ysend.at[c, k], yrecv.at[c, k], ypeer(k))

    def zcopy(c, s):
        at = pl.ds(*CHUNKS[c])
        return remote(at_ref.at[at], za.at[s, at], zsend.at[c, s], zrecv.at[c, s], device(arc, x, zh, y, goes[s]))

    def send_z(c, s):
        if s == 0:
            zcopy(c, 0).start()
        else:
            @pl.when(odd)
            def _():
                zcopy(c, 1).start()

    def send_y(c, ks):
        for k in ks:
            ycopy(c, k).start()

    def weigh(src, dst, c):
        first, rows = CHUNKS[c]

        def chunk(i, carry):
            at = pl.ds(pl.multiple_of(first + i * 32, 32), 32)
            dst[at, :] = (src[at, :].astype(F32) * w_ref[...]).astype(BF16)
            return carry

        lax.fori_loop(0, rows // 32, chunk, 0)

    def take_z(c, s):
        def go():
            zcopy(c, s).wait_recv()
            weigh(za.at[s], zw.at[s], c)

        if s == 0:
            go()
        else:
            pl.when(even)(go)

    def take_y(c, ks):
        for k in ks:
            yarrival(c, k).wait_recv()
            weigh(ya.at[back(y, k)], yw.at[back(y, k)], c)

    near, far = (1, 3), (2,)
    send_z(0, 0)
    send_y(0, near)
    send_z(0, 1)
    send_y(0, far)
    ya[y] = at_ref[...]
    for c in range(len(CHUNKS)):
        weigh(at_ref, yw.at[y], c)

    def nt(a, b):
        return lax.dot_general(a, b, (((1,), (1,)), ((), ())), preferred_element_type=F32)

    take_z(0, 0)
    take_y(0, near)
    take_z(0, 1)
    take_y(0, far)
    send_z(1, 0)
    send_y(1, near)
    send_z(2, 0)
    send_y(2, near)
    ahead_w = yw[:, 0:64, :].reshape(256, obs)
    strip[0] = 0.5 * nt(at_ref[0:64, :], ahead_w)
    ahead_a = ya[:, 0:64, :].reshape(256, obs)
    strip[1] = 0.5 * (nt(za[0, 0:64, :], ahead_w) + nt(zw[0, 0:64, :], ahead_a))

    @pl.when(even)
    def _():
        strip[2] = 0.5 * (nt(za[1, 0:64, :], yw[:, 0:64, :].reshape(256, obs)) + nt(zw[1, 0:64, :], ya[:, 0:64, :].reshape(256, obs)))

    @pl.when(odd)
    def _():
        strip[2] = jnp.zeros((64, 256), F32)

    theirs = pl.ds(pl.multiple_of((1 - arc) * 32, 32), 32)
    ours = pl.ds(pl.multiple_of(arc * 32, 32), 32)
    s1 = remote(strip.at[:, theirs], sbuf, s1s, s1r, mate)
    s1.start()
    s1.wait()
    mine[...] = strip[:, ours] + sbuf[...]
    def share(k):
        return pl.ds(pl.multiple_of(((x + k) % 4) * 8, 8), 8)

    own = share(0)
    s2 = [remote(mine.at[:, share(k)], sx.at[x], s2s.at[k], s2r.at[k], xpeer(k)) for k in turns]
    for c in s2:
        c.start()
    sx[x] = mine[:, own]
    for c in s2:
        c.wait()
    sz[zh] = (sx[0] + sx[1]) + (sx[2] + sx[3])
    s3 = remote(sz.at[zh], sz.at[zh], s3s, s3r, zpeer)
    s3.start()
    s3.wait()
    sums = sz[0] + sz[1]
    lane = lax.broadcasted_iota(jnp.int32, (8, 256), 1)
    sub = lax.broadcasted_iota(jnp.int32, (8, 256), 0)
    prior4 = jnp.concatenate([prior_ref[0]] * 4, axis=1)
    diagonal = jnp.where(lane == y * 64 + arc * 32 + x * 8 + sub, 0.5 * prior4, 0.0)
    seen[arc, y, zl, 0, own] = sums[0] + diagonal
    seen[arc, y, zl, 1, own] = sums[1]
    seen[arc, y, zl, 2, own] = sums[2]
    view = seen.at[arc, y, zl, :, own]
    s4 = [remote(view, view, s4s.at[k], s4r.at[k], lpeer(k)) for k in turns]
    for c in s4:
        c.start()
    for c in s4:
        c.wait()
    low, high = pl.ds(0, 2), pl.ds(2, 2)

    def both_ways(first, second, send, recv):
        return ([remote(first, first, send.at[0, k], recv.at[0, k], xpeer(k)) for k in turns]
                + [remote(second, second, send.at[1, k], recv.at[1, k], ypeer(k)) for k in turns])

    s5 = both_ways(seen.at[arc, y, low, :, own], seen.at[arc, y, high, :, own], s5s, s5r)
    for c in s5:
        c.start()
    for c in s5:
        c.wait()
    s6 = both_ways(seen.at[arc, :, high, :, own], seen.at[arc, y, low], s6s, s6r)
    for c in s6:
        c.start()
    send_z(1, 1)
    send_y(1, far)
    send_z(2, 1)
    send_y(2, far)
    s7 = remote(seen.at[arc], seen.at[arc], s7s, s7r, mate)

    def trade(g):
        first, n = GROUPS[g]
        return remote(part.at[pl.ds(first, n), pl.ds(pl.multiple_of((1 - arc) * half, half), half)],
                      dbuf.at[pl.ds(first, n)], dsend.at[g], drecv.at[g], mate)

    def products(first, n, kind, slot, shift):
        def one(i, carry):
            k = (y + shift(i)) % 4
            if kind == "own":
                part[first + i] = nt(at_ref[...], yw[k])
            elif kind == "rows":
                part[first + i] = nt(za[slot], yw[k])
            else:
                part[first + i] = nt(ya[k], zw[slot])
            return carry

        lax.fori_loop(0, n, one, 0)

    def first_products():
        for c in (1, 2):
            take_y(c, near)
            take_z(c, 0)
        for i, kind in enumerate(("own", "rows", "cols")):
            products(3 * i, 3, kind, 0, lambda i: i + jnp.where(i == 2, 1, 0))
        trade(0).start()

    def last_products():
        for c in (1, 2):
            take_y(c, far)
            take_z(c, 1)
        for i, kind in enumerate(("own", "rows", "cols")):
            products(9 + i, 1, kind, 0, lambda i: 2)
        trade(1).start()

        @pl.when(even)
        def _():
            products(12, 4, "rows", 1, lambda i: i)
            products(16, 4, "cols", 1, lambda i: i)
            trade(2).start()

    def fspread(g, k):
        first, n = GROUPS[g]
        at = pl.ds(pl.multiple_of(arc * half + ((x + k) % 4) * piece, 16), piece)
        return remote(part.at[pl.ds(first, n), at, pl.ds(0, 128)], xf.at[k - 1, pl.ds(first, n)],
                      fxs.at[k, g], fxr.at[k, g], xpeer(k))

    def bspread(g, k):
        first, n = GROUPS[g]
        at = pl.ds(pl.multiple_of(((x + k) % 4) * piece, 16), piece)
        return remote(narrow.at[pl.ds(first, n), at], xb.at[k - 1, pl.ds(first, n)],
                      bxs.at[k, g], bxr.at[k, g], xpeer(k))

    def halves(g):
        first, n = GROUPS[g]
        trade(g).wait()
        rows = pl.ds(pl.multiple_of(arc * half, half), half)

        def add(b, carry):
            both = part[first + b, rows] + dbuf[first + b]
            part[first + b, rows] = both
            narrow[first + b] = both[:, 128:].astype(BF16)
            return carry

        lax.fori_loop(0, n, add, 0)
        for k in turns:
            fspread(g, k).start()

    def spread_rest(g):
        for k in turns:
            bspread(g, k).start()

    lanes = (pl.ds(0, 128), pl.ds(128, size - 128))

    def final(b, w, act):
        target, upper, here = owner(blocks[b])
        src = part.at[b, pl.ds(pl.multiple_of(arc * half + x * piece, 16), piece), lanes[w]]
        dst = fbuf.at[upper, zh, x, :, lanes[w]]
        sem = frecv.at[w, upper, zh, x]

        @pl.when(here)
        def _():
            if act == "start":
                pltpu.make_async_copy(src, dst, sem).start()

        @pl.when(jnp.logical_not(here))
        def _():
            c = remote(src, dst, fsend.at[w, b], sem, target)
            if act == "start":
                c.start()
            else:
                c.wait_send()

    def deliver(g, w):
        first, n = GROUPS[g]
        rows = pl.ds(pl.multiple_of(arc * half + x * piece, 16), piece)
        spread, landed = (fspread, xf) if w == 0 else (bspread, xb)
        for k in turns:
            spread(g, k).wait()

        def add(b, carry):
            at = first + b
            part[at, rows, lanes[w]] = ((part[at, rows, lanes[w]] + landed[0, at].astype(F32))
                                      + (landed[1, at].astype(F32) + landed[2, at].astype(F32)))
            return carry

        lax.fori_loop(0, n, add, 0)
        for b in range(first, first + n):
            final(b, w, "start")

    def both(f, *rest):
        f(1, *rest)

        @pl.when(even)
        def _():
            f(2, *rest)

    prior_row = jnp.concatenate([prior_ref[k] for k in range(6)], axis=1)

    def collect(w):
        width = lanes[w].size
        lane = lax.broadcasted_iota(jnp.int32, (piece, width), 1) + lanes[w].start
        sub = lax.broadcasted_iota(jnp.int32, (piece, width), 0)
        for upper in range(2):
            for xx in range(4):
                for zz in range(2):
                    pltpu.make_async_copy(part.at[0, pl.ds(0, piece), lanes[w]], fbuf.at[upper, zz, xx, :, lanes[w]],
                                          frecv.at[w, upper, zz, xx]).wait()
                first = arc * half + xx * piece
                at = pl.ds(pl.multiple_of(first, 16), piece)
                hit = (lane == sub + first) & (col == row + 8 * upper)
                out_ref[upper, at, lanes[w]] = ((fbuf[upper, 0, xx, :, lanes[w]] + fbuf[upper, 1, xx, :, lanes[w]])
                                                + jnp.where(hit, prior_row[:, lanes[w].start : lanes[w].start + width], 0.0))

    def swap_out(w):
        view = out_ref.at[:, pl.ds(pl.multiple_of(arc * half, half), half), lanes[w]]
        return remote(view, view, osend.at[w], orecv.at[w], mate)

    lead = gt.at[arc, col]
    gz = [remote(lead, lead, gzs.at[k], gzr.at[k], lpeer(k)) for k in turns]
    view = gt.at[arc, pl.ds(y * 4, 4)]
    gy = [remote(view, view, gys.at[k], gyr.at[k], ypeer(k)) for k in turns]
    gc = remote(gt.at[arc], gt.at[arc], gcs, gcr, mate)

    first_products()
    for c in s6:
        c.wait()
    s7.start()
    halves(0)
    spread_rest(0)
    s7.wait()
    hosts = {0: (0, 1, 3), 1: (1, 3), 2: (2, 0, 1), 3: (3, 2)}

    def assemble(t, carry):
        a, yy = t // 4, t % 4
        for z1 in range(4):
            at = pl.ds(pl.multiple_of(yy * 256 + z1 * 64 + a * 32, 32), 32)
            for pair in range(2):
                sides = []
                for z2 in (2 * pair, 2 * pair + 1):
                    sides.append(seen[a, yy, z2, hosts[z2].index(z1)] if z1 in hosts[z2] else jnp.zeros((32, 256), F32))
                for y2 in range(4):
                    cut = slice(y2 * 64, y2 * 64 + 64)
                    v[at, y2 * 256 + pair * 128 : y2 * 256 + pair * 128 + 128] = jnp.concatenate(
                        [sides[0][:, cut], sides[1][:, cut]], axis=1)
        return carry

    lax.fori_loop(0, 8, assemble, 0)

    def symmetric(i, carry):
        at = pl.ds(pl.multiple_of(i * 128, 128), 128)

        def one(j, carry):
            here = pl.ds(pl.multiple_of(j * 128, 128), 128)
            whole = v[at, here] + v[here, at].T
            v[at, here] = whole
            v[here, at] = whole.T
            return carry

        return lax.fori_loop(i, 8, one, carry)

    lax.fori_loop(0, 8, symmetric, 0)

    def split(m):
        first = m.astype(BF16)
        rest = m - first.astype(F32)
        second = rest.astype(BF16)
        return first, second, (rest - second.astype(F32)).astype(BF16)

    def left_parts(m):
        a, b, c = split(m)
        return jnp.concatenate([a, b, a, b, a, c], axis=1)

    def right_parts(m):
        a, b, c = split(m)
        for i, q in enumerate((a, b, b, a, c, a)):
            rcat[i * 128 : i * 128 + 128, :] = q

    def step(p, carry):
        @pl.when(p == 1)
        def _():
            last_products()

        @pl.when(p == 2)
        def _():
            deliver(0, 0)
            deliver(0, 1)

        @pl.when(p == 4)
        def _():
            both(deliver, 0)

        @pl.when(p == 6)
        def _():
            collect(0)
            rows = pl.ds(pl.multiple_of(arc * half, half), half)
            for upper in range(2):
                gt[arc, col, :, upper * half : upper * half + half] = out_ref[upper, rows, 0:128].T[0:64, :]
            for c in gz:
                c.start()
            swap_out(0).start()

        @pl.when(p == 7)
        def _():
            both(deliver, 1)

        b = 128
        at = pl.ds(pl.multiple_of(p * b, b), b)
        inv = factor_inverse(v[at, at])

        @pl.when(p == 1)
        def _():
            both(halves)
            both(spread_rest)

        v[at, at] = jnp.eye(b, dtype=F32)
        right_parts(v[at, :])
        whole = jnp.dot(left_parts(inv), rcat[...], preferred_element_type=F32)
        v[at, :] = whole
        right_parts(whole)

        def below(i, carry):
            here = pl.ds(pl.multiple_of(i * b, b), b)
            left = left_parts(v[at, here].T)
            v[here, at] = jnp.zeros((b, b), F32)
            v[here, :] = v[here, :] - jnp.dot(left, rcat[...], preferred_element_type=F32)
            return carry

        lax.fori_loop(p + 1, 8, below, 0)
        return carry

    lax.fori_loop(0, 8, step, 0)
    for j in range(4):
        v[j * 256 : j * 256 + 128, j * 256 + 128 : j * 256 + 256] = jnp.zeros((128, 128), F32)

    for c in gz:
        c.wait()
    for c in gy:
        c.start()
    collect(1)
    swap_out(1).start()
    for c in gy:
        c.wait()
    gc.start()
    for w in range(2):
        swap_out(w).wait()
    for upper in range(2):
        for kr in range(6):
            for kc in range(6):
                norm_ref[pl.ds((2 * kr + upper) * 384 + kc, 64, stride=6), :] = out_ref[
                    upper, kr * 64 : kr * 64 + 64, kc * 64 : kc * 64 + 64]
    gc.wait()

    def panel(j, carry):
        at = pl.ds(pl.multiple_of(j * 256, 256), 256)

        def one(k, carry):
            here = pl.ds(pl.multiple_of(k * 256, 256), 256)
            return tuple(carry[a] + jnp.dot(v[at, here], gt[a, pl.ds(k * 4, 4)].reshape(256, size),
                                            precision=HIGHEST, preferred_element_type=F32) for a in range(2))

        both = lax.fori_loop(0, j + 1, one, (jnp.zeros((256, size), F32),) * 2)
        for a in range(2):
            turned = both[a].T
            for upper in range(2):
                for kc in range(3):
                    tile = 2 * (a * 3 + kc) + upper
                    panel_ref[tile * 64 : tile * 64 + 64, at] = turned[upper * half + kc * 64 : upper * half + kc * 64 + 64]
        return carry

    lax.fori_loop(0, 4, panel, 0)

    for c in range(len(CHUNKS)):
        zcopy(c, 0).wait_send()

        @pl.when(odd)
        def _():
            zcopy(c, 1).wait_send()

        for k in turns:
            ycopy(c, k).wait_send()
    for w in range(2):
        for b in range(12):
            final(b, w, "end")

        @pl.when(even)
        def _():
            for b in range(12, 20):
                final(b, w, "end")


def normal_and_panel(at, weight, prior):
    size, obs = at.shape
    dma = pltpu.SemaphoreType.DMA
    n = len(CHUNKS)
    return pl.pallas_call(
        kernel,
        out_shape=(jax.ShapeDtypeStruct((12 * size, 64), F32), jax.ShapeDtypeStruct((2 * size, 1024), F32)),
        in_specs=[VMEM] * 3,
        out_specs=(VMEM, VMEM),
        scratch_shapes=[
            pltpu.VMEM((2, size, size), F32),
            pltpu.VMEM((4, size, obs), BF16),
            pltpu.VMEM((2, size, obs), BF16),
            pltpu.VMEM((4, size, obs), BF16),
            pltpu.VMEM((2, size, obs), BF16),
            pltpu.VMEM((20, size, size), F32),
            pltpu.VMEM((20, size // 2, size), F32),
            pltpu.VMEM((20, size // 2, size - 128), BF16),
            pltpu.VMEM((3, 20, size // 8, 128), F32),
            pltpu.VMEM((3, 20, size // 8, size - 128), BF16),
            pltpu.VMEM((2, 2, 4, size // 8, size), F32),
            pltpu.VMEM((3, 64, 256), F32),
            pltpu.VMEM((3, 32, 256), F32),
            pltpu.VMEM((3, 32, 256), F32),
            pltpu.VMEM((4, 3, 8, 256), F32),
            pltpu.VMEM((2, 3, 8, 256), F32),
            pltpu.VMEM((2, 4, 4, 3, 32, 256), F32),
            pltpu.VMEM((1024, 1024), F32),
            pltpu.VMEM((768, 1024), BF16),
            pltpu.VMEM((2, 16, 64, size), F32),
            dma((n, 4)), dma((n, 4)), dma((n, 2)), dma((n, 2)), dma((3,)), dma((3,)),
            dma((4, 3)), dma((4, 3)), dma((4, 3)), dma((4, 3)), dma((2, 20)), dma((2, 2, 2, 4)), dma((2,)), dma((2,)),
            dma, dma, dma((4,)), dma((4,)), dma, dma, dma((4,)), dma((4,)), dma((2, 4)), dma((2, 4)), dma((2, 4)), dma((2, 4)), dma, dma,
            dma((4,)), dma((4,)), dma((4,)), dma((4,)), dma, dma,
        ],
        compiler_params=pltpu.CompilerParams(collective_id=0, has_side_effects=True, vmem_limit_bytes=60 << 20),
        name="normal_and_panel",
    )(at, weight, prior)


def body(design, obs_weight, prior):
    rows_dev, kc_tiles, single, tile = design.shape
    local_cols = kc_tiles * tile
    normal, panel = normal_and_panel(
        design.transpose(1, 2, 3, 0).reshape(local_cols, rows_dev), obs_weight.reshape(1, rows_dev), prior)
    shape = (2 * kc_tiles, 1, tile, kc_tiles, 1, tile)
    return (normal.reshape(shape), panel.reshape(2 * kc_tiles, 1, tile, 1024))


def solution(mesh):
    placed = (P(("arc", "row"), None, "col", None), P(("arc", "row")), P(None, "col", None))
    return jax.shard_map(
        body,
        mesh=mesh,
        in_specs=placed,
        out_specs=(P(None, "row", None, None, "col", None), P(None, "row", None, None)),
        check_vma=False,
    )
```

```python
import functools

import jax
import jax.numpy as jnp
from jax import lax
from jax.experimental import pallas as pl
from jax.experimental.pallas import tpu as pltpu
from jax.sharding import PartitionSpec as P

F32 = jnp.float32
BF16 = jnp.bfloat16
MESH = pl.DeviceIdType.MESH
VMEM = pl.BlockSpec(memory_space=pltpu.VMEM)
HIGHEST = lax.Precision.HIGHEST


def place():
    arc = lax.axis_index("arc")
    row = lax.axis_index("row")
    col = lax.axis_index("col")
    return arc, row // 2, row % 2, col // 4, col % 4


def device(arc, x, zh, y, zl):
    return (arc, x * 2 + zh, y * 4 + zl)


def pick(values, at):
    out = jnp.int32(values[0])
    for k in range(1, len(values)):
        out = jnp.where(at == k, values[k], out)
    return out


def factor_inverse(block):
    n = block.shape[0]
    lane = lax.broadcasted_iota(jnp.int32, (8, n), 1)
    sub = lax.broadcasted_iota(jnp.int32, (8, n), 0)
    groups = [block[8 * g : 8 * g + 8, :] for g in range(n // 8)]
    for q in range(n // 8):
        pivot = groups[q]
        inside = (lane >= 8 * q) & (lane < 8 * q + 8)
        cols = [jnp.broadcast_to(pivot[:, 8 * q + j : 8 * q + j + 1], (8, n)) for j in range(8)]
        rows = jnp.where(inside, (lane - 8 * q == sub).astype(F32), pivot)
        scale, mult, scaled = [], {}, []
        for j in range(8):
            r = lax.rsqrt(cols[j][j : j + 1, :])
            scale.append(r)
            m = jnp.where(sub > j, cols[j] * r, 0.0)
            for l in range(j + 1, 8):
                mult[j, l] = cols[l][j : j + 1, :] * r
                cols[l] = cols[l] - m * mult[j, l]
            top = rows[j : j + 1, :] * r
            scaled.append(top)
            rows = jnp.where(sub == j, top, rows - m * top)
        groups[q] = rows
        for g in range(q + 1, n // 8):
            low = groups[g]
            c = [jnp.broadcast_to(low[:, 8 * q + j : 8 * q + j + 1], (8, n)) for j in range(8)]
            low = jnp.where(inside, 0.0, low)
            for j in range(8):
                m = c[j] * scale[j]
                for l in range(j + 1, 8):
                    c[l] = c[l] - m * mult[j, l]
                low = low - m * scaled[j]
            groups[g] = low
    lane_all = lax.broadcasted_iota(jnp.int32, (n, n), 1)
    sub_all = lax.broadcasted_iota(jnp.int32, (n, n), 0)
    return jnp.where(lane_all <= sub_all, jnp.concatenate(groups, axis=0), 0.0)


CHUNKS = ((0, 64), (64, 128), (192, 192))
GROUPS = ((0, 9), (9, 3), (12, 8))


def kernel(at_ref, w_ref, prior_ref, norm_ref, panel_ref, out_ref,
           ya, za, yw, zw, part, dbuf, narrow, xf, xb, fbuf, strip, sbuf, mine, sx, sz, seen, v, rcat, gt,
           ysend, yrecv, zsend, zrecv, dsend, drecv, fxs, fxr, bxs, bxr, fsend, frecv, osend, orecv,
           s1s, s1r, s2s, s2r, s3s, s3r, s4s, s4r, s5s, s5r, s6s, s6r, s7s, s7r, gzs, gzr, gys, gyr, gcs, gcr):
    arc, x, zh, y, zl = place()
    size, obs = at_ref.shape
    half, piece = size // 2, size // 8
    even = zl % 2 == 0
    odd = jnp.logical_not(even)
    moved = (pick((1, 3, 0, 2), zl), pick((3, 0, 1, 0), zl))
    goes = (pick((2, 0, 3, 1), zl), pick((0, 2, 0, 0), zl))
    mate = device(1 - arc, x, zh, y, zl)
    zpeer = device(arc, x, 1 - zh, y, zl)
    col, row = y * 4 + zl, x * 2 + zh
    turns = (1, 3, 2)

    def xpeer(k):
        return device(arc, (x + k) % 4, zh, y, zl)

    def ypeer(k):
        return device(arc, x, zh, (y + k) % 4, zl)

    def lpeer(k):
        return device(arc, x, zh, y, (zl + k) % 4)

    def back(at, k):
        return (at + 4 - k) % 4

    def remote(src, dst, send, recv, target):
        return pltpu.make_async_remote_copy(src, dst, send, recv, device_id=target, device_id_type=MESH)

    blocks = [(kind, 0, k) for kind in ("own", "rows", "cols") for k in (0, 1, 3)]
    blocks += [(kind, 0, 2) for kind in ("own", "rows", "cols")]
    blocks += [(kind, 1, k) for kind in ("rows", "cols") for k in range(4)]

    def owner(block):
        kind, slot, k = block
        k = (y + k) % 4
        if kind == "own":
            y1, z1, y2, z2 = y, zl, k, zl
        elif kind == "rows":
            y1, z1, y2, z2 = y, moved[slot], k, zl
        else:
            y1, z1, y2, z2 = k, zl, y, moved[slot]
        r = (y1 % 2) * 4 + z1
        here = (r == row) & (y2 == y) & (z2 == zl)
        return (arc, r, y2 * 4 + z2), y1 // 2, here

    bar = pltpu.get_barrier_semaphore()

    def greet(target):
        pl.semaphore_signal(bar, inc=1, device_id=target, device_id_type=MESH)

    for k in turns:
        greet(ypeer(k))
        greet(xpeer(k))
        greet(lpeer(k))
    greet(mate)
    greet(zpeer)
    pl.semaphore_wait(bar, 11)

    def ycopy(c, k):
        at = pl.ds(*CHUNKS[c])
        return remote(at_ref.at[at], ya.at[y, at], ysend.at[c, k], yrecv.at[c, k], ypeer(k))

    def yarrival(c, k):
        at = pl.ds(*CHUNKS[c])
        return remote(at_ref.at[at], ya.at[back(y, k), at], ysend.at[c, k], yrecv.at[c, k], ypeer(k))

    def zcopy(c, s):
        at = pl.ds(*CHUNKS[c])
        return remote(at_ref.at[at], za.at[s, at], zsend.at[c, s], zrecv.at[c, s], device(arc, x, zh, y, goes[s]))

    def send_z(c, s):
        if s == 0:
            zcopy(c, 0).start()
        else:
            @pl.when(odd)
            def _():
                zcopy(c, 1).start()

    def send_y(c, ks):
        for k in ks:
            ycopy(c, k).start()

    def weigh(src, dst, c):
        first, rows = CHUNKS[c]

        def chunk(i, carry):
            at = pl.ds(pl.multiple_of(first + i * 32, 32), 32)
            dst[at, :] = (src[at, :].astype(F32) * w_ref[...]).astype(BF16)
            return carry

        lax.fori_loop(0, rows // 32, chunk, 0)

    def take_z(c, s):
        def go():
            zcopy(c, s).wait_recv()
            weigh(za.at[s], zw.at[s], c)

        if s == 0:
            go()
        else:
            pl.when(even)(go)

    def take_y(c, ks):
        for k in ks:
            yarrival(c, k).wait_recv()
            weigh(ya.at[back(y, k)], yw.at[back(y, k)], c)

    near, far = (1, 3), (2,)
    send_z(0, 0)
    send_y(0, near)
    send_z(0, 1)
    send_y(0, far)
    ya[y] = at_ref[...]
    for c in range(len(CHUNKS)):
        weigh(at_ref, yw.at[y], c)

    def nt(a, b):
        return lax.dot_general(a, b, (((1,), (1,)), ((), ())), preferred_element_type=F32)

    take_z(0, 0)
    take_y(0, near)
    take_z(0, 1)
    take_y(0, far)
    send_z(1, 0)
    send_y(1, near)
    ahead_w = yw[:, 0:64, :].reshape(256, obs)
    strip[0] = 0.5 * nt(at_ref[0:64, :], ahead_w)
    ahead_a = ya[:, 0:64, :].reshape(256, obs)
    strip[1] = 0.5 * (nt(za[0, 0:64, :], ahead_w) + nt(zw[0, 0:64, :], ahead_a))

    @pl.when(even)
    def _():
        strip[2] = 0.5 * (nt(za[1, 0:64, :], yw[:, 0:64, :].reshape(256, obs)) + nt(zw[1, 0:64, :], ya[:, 0:64, :].reshape(256, obs)))

    @pl.when(odd)
    def _():
        strip[2] = jnp.zeros((64, 256), F32)

    theirs = pl.ds(pl.multiple_of((1 - arc) * 32, 32), 32)
    ours = pl.ds(pl.multiple_of(arc * 32, 32), 32)
    s1 = remote(strip.at[:, theirs], sbuf, s1s, s1r, mate)
    s1.start()
    s1.wait()
    mine[...] = strip[:, ours] + sbuf[...]
    def share(k):
        return pl.ds(pl.multiple_of(((x + k) % 4) * 8, 8), 8)

    own = share(0)
    s2 = [remote(mine.at[:, share(k)], sx.at[x], s2s.at[k], s2r.at[k], xpeer(k)) for k in turns]
    for c in s2:
        c.start()
    sx[x] = mine[:, own]
    for c in s2:
        c.wait()
    sz[zh] = (sx[0] + sx[1]) + (sx[2] + sx[3])
    send_y(2, near)
    s3 = remote(sz.at[zh], sz.at[zh], s3s, s3r, zpeer)
    s3.start()
    s3.wait()
    sums = sz[0] + sz[1]
    lane = lax.broadcasted_iota(jnp.int32, (8, 256), 1)
    sub = lax.broadcasted_iota(jnp.int32, (8, 256), 0)
    prior4 = jnp.concatenate([prior_ref[0]] * 4, axis=1)
    diagonal = jnp.where(lane == y * 64 + arc * 32 + x * 8 + sub, 0.5 * prior4, 0.0)
    seen[arc, y, zl, 0, own] = sums[0] + diagonal
    seen[arc, y, zl, 1, own] = sums[1]
    seen[arc, y, zl, 2, own] = sums[2]
    view = seen.at[arc, y, zl, :, own]
    s4 = [remote(view, view, s4s.at[k], s4r.at[k], lpeer(k)) for k in turns]
    for c in s4:
        c.start()
    for c in s4:
        c.wait()
    low, high = pl.ds(0, 2), pl.ds(2, 2)

    def both_ways(first, second, send, recv):
        return ([remote(first, first, send.at[0, k], recv.at[0, k], xpeer(k)) for k in turns]
                + [remote(second, second, send.at[1, k], recv.at[1, k], ypeer(k)) for k in turns])

    s5 = both_ways(seen.at[arc, y, low, :, own], seen.at[arc, y, high, :, own], s5s, s5r)
    for c in s5:
        c.start()
    send_z(2, 0)
    for c in s5:
        c.wait()
    s6 = both_ways(seen.at[arc, :, high, :, own], seen.at[arc, y, low], s6s, s6r)
    for c in s6:
        c.start()
    send_z(1, 1)
    send_z(2, 1)
    send_y(1, far)
    send_y(2, far)
    s7 = remote(seen.at[arc], seen.at[arc], s7s, s7r, mate)

    def trade(g):
        first, n = GROUPS[g]
        return remote(part.at[pl.ds(first, n), pl.ds(pl.multiple_of((1 - arc) * half, half), half)],
                      dbuf.at[pl.ds(first, n)], dsend.at[g], drecv.at[g], mate)

    def products(first, n, kind, slot, shift):
        def one(i, carry):
            k = (y + shift(i)) % 4
            if kind == "own":
                part[first + i] = nt(at_ref[...], yw[k])
            elif kind == "rows":
                part[first + i] = nt(za[slot], yw[k])
            else:
                part[first + i] = nt(ya[k], zw[slot])
            return carry

        lax.fori_loop(0, n, one, 0)

    def first_products():
        for c in (1, 2):
            take_y(c, near)
            take_z(c, 0)
        for i, kind in enumerate(("own", "rows", "cols")):
            products(3 * i, 3, kind, 0, lambda i: i + jnp.where(i == 2, 1, 0))
        trade(0).start()

    def last_products():
        for c in (1, 2):
            take_y(c, far)
            take_z(c, 1)
        for i, kind in enumerate(("own", "rows", "cols")):
            products(9 + i, 1, kind, 0, lambda i: 2)
        trade(1).start()

        @pl.when(even)
        def _():
            products(12, 4, "rows", 1, lambda i: i)
            products(16, 4, "cols", 1, lambda i: i)
            trade(2).start()

    def fspread(g, k):
        first, n = GROUPS[g]
        at = pl.ds(pl.multiple_of(arc * half + ((x + k) % 4) * piece, 16), piece)
        return remote(part.at[pl.ds(first, n), at, pl.ds(0, 128)], xf.at[k - 1, pl.ds(first, n)],
                      fxs.at[k, g], fxr.at[k, g], xpeer(k))

    def bspread(g, k):
        first, n = GROUPS[g]
        at = pl.ds(pl.multiple_of(((x + k) % 4) * piece, 16), piece)
        return remote(narrow.at[pl.ds(first, n), at], xb.at[k - 1, pl.ds(first, n)],
                      bxs.at[k, g], bxr.at[k, g], xpeer(k))

    def halves(g):
        first, n = GROUPS[g]
        trade(g).wait()
        rows = pl.ds(pl.multiple_of(arc * half, half), half)

        def add(b, carry):
            both = part[first + b, rows] + dbuf[first + b]
            part[first + b, rows] = both
            narrow[first + b] = both[:, 128:].astype(BF16)
            return carry

        lax.fori_loop(0, n, add, 0)
        for k in turns:
            fspread(g, k).start()

    def spread_rest(g):
        for k in turns:
            bspread(g, k).start()

    lanes = (pl.ds(0, 128), pl.ds(128, size - 128))

    def final(b, w, act):
        target, upper, here = owner(blocks[b])
        src = part.at[b, pl.ds(pl.multiple_of(arc * half + x * piece, 16), piece), lanes[w]]
        dst = fbuf.at[upper, zh, x, :, lanes[w]]
        sem = frecv.at[w, upper, zh, x]

        @pl.when(here)
        def _():
            if act == "start":
                pltpu.make_async_copy(src, dst, sem).start()

        @pl.when(jnp.logical_not(here))
        def _():
            c = remote(src, dst, fsend.at[w, b], sem, target)
            if act == "start":
                c.start()
            else:
                c.wait_send()

    def deliver(g, w):
        first, n = GROUPS[g]
        rows = pl.ds(pl.multiple_of(arc * half + x * piece, 16), piece)
        spread, landed = (fspread, xf) if w == 0 else (bspread, xb)
        for k in turns:
            spread(g, k).wait()

        def add(b, carry):
            at = first + b
            part[at, rows, lanes[w]] = ((part[at, rows, lanes[w]] + landed[0, at].astype(F32))
                                      + (landed[1, at].astype(F32) + landed[2, at].astype(F32)))
            return carry

        lax.fori_loop(0, n, add, 0)
        for b in range(first, first + n):
            final(b, w, "start")

    def both(f, *rest):
        f(1, *rest)

        @pl.when(even)
        def _():
            f(2, *rest)

    prior_row = jnp.concatenate([prior_ref[k] for k in range(6)], axis=1)

    def collect(w):
        width = lanes[w].size
        lane = lax.broadcasted_iota(jnp.int32, (piece, width), 1) + lanes[w].start
        sub = lax.broadcasted_iota(jnp.int32, (piece, width), 0)
        for upper in range(2):
            for xx in range(4):
                for zz in range(2):
                    pltpu.make_async_copy(part.at[0, pl.ds(0, piece), lanes[w]], fbuf.at[upper, zz, xx, :, lanes[w]],
                                          frecv.at[w, upper, zz, xx]).wait()
                first = arc * half + xx * piece
                at = pl.ds(pl.multiple_of(first, 16), piece)
                hit = (lane == sub + first) & (col == row + 8 * upper)
                out_ref[upper, at, lanes[w]] = ((fbuf[upper, 0, xx, :, lanes[w]] + fbuf[upper, 1, xx, :, lanes[w]])
                                                + jnp.where(hit, prior_row[:, lanes[w].start : lanes[w].start + width], 0.0))

    def swap_out(w):
        view = out_ref.at[:, pl.ds(pl.multiple_of(arc * half, half), half), lanes[w]]
        return remote(view, view, osend.at[w], orecv.at[w], mate)

    lead = gt.at[arc, col]
    gz = [remote(lead, lead, gzs.at[k], gzr.at[k], lpeer(k)) for k in turns]
    view = gt.at[arc, pl.ds(y * 4, 4)]
    gy = [remote(view, view, gys.at[k], gyr.at[k], ypeer(k)) for k in turns]
    gc = remote(gt.at[arc], gt.at[arc], gcs, gcr, mate)

    first_products()
    for c in s6:
        c.wait()
    s7.start()
    halves(0)
    spread_rest(0)
    s7.wait()
    hosts = {0: (0, 1, 3), 1: (1, 3), 2: (2, 0, 1), 3: (3, 2)}

    def assemble(t, carry):
        a, yy = t // 4, t % 4
        for z1 in range(4):
            at = pl.ds(pl.multiple_of(yy * 256 + z1 * 64 + a * 32, 32), 32)
            for pair in range(2):
                sides = []
                for z2 in (2 * pair, 2 * pair + 1):
                    sides.append(seen[a, yy, z2, hosts[z2].index(z1)] if z1 in hosts[z2] else jnp.zeros((32, 256), F32))
                for y2 in range(4):
                    cut = slice(y2 * 64, y2 * 64 + 64)
                    v[at, y2 * 256 + pair * 128 : y2 * 256 + pair * 128 + 128] = jnp.concatenate(
                        [sides[0][:, cut], sides[1][:, cut]], axis=1)
        return carry

    lax.fori_loop(0, 8, assemble, 0)

    def symmetric(i, carry):
        at = pl.ds(pl.multiple_of(i * 128, 128), 128)

        def one(j, carry):
            here = pl.ds(pl.multiple_of(j * 128, 128), 128)
            whole = v[at, here] + v[here, at].T
            v[at, here] = whole
            v[here, at] = whole.T
            return carry

        return lax.fori_loop(i, 8, one, carry)

    lax.fori_loop(0, 8, symmetric, 0)

    def split(m):
        first = m.astype(BF16)
        rest = m - first.astype(F32)
        second = rest.astype(BF16)
        return first, second, (rest - second.astype(F32)).astype(BF16)

    def left_parts(m):
        a, b, c = split(m)
        return jnp.concatenate([a, b, a, b, a, c], axis=1)

    def right_parts(m):
        a, b, c = split(m)
        for i, q in enumerate((a, b, b, a, c, a)):
            rcat[i * 128 : i * 128 + 128, :] = q

    def step(p, carry):
        @pl.when(p == 1)
        def _():
            deliver(0, 0)
            last_products()

        @pl.when(p == 3)
        def _():
            both(deliver, 0)
            both(spread_rest)
            deliver(0, 1)

        @pl.when(p == 4)
        def _():
            collect(0)
            rows = pl.ds(pl.multiple_of(arc * half, half), half)
            for upper in range(2):
                gt[arc, col, :, upper * half : upper * half + half] = out_ref[upper, rows, 0:128].T[0:64, :]
            for c in gz:
                c.start()
            swap_out(0).start()

        @pl.when(p == 5)
        def _():
            for c in gz:
                c.wait()
            for c in gy:
                c.start()
            both(deliver, 1)

        b = 128
        at = pl.ds(pl.multiple_of(p * b, b), b)
        inv = factor_inverse(v[at, at])

        @pl.when(p == 1)
        def _():
            both(halves)

        v[at, at] = jnp.eye(b, dtype=F32)
        right_parts(v[at, :])
        whole = jnp.dot(left_parts(inv), rcat[...], preferred_element_type=F32)
        v[at, :] = whole
        right_parts(whole)

        def below(i, carry):
            here = pl.ds(pl.multiple_of(i * b, b), b)
            left = left_parts(v[at, here].T)
            v[here, at] = jnp.zeros((b, b), F32)
            v[here, :] = v[here, :] - jnp.dot(left, rcat[...], preferred_element_type=F32)
            return carry

        lax.fori_loop(p + 1, 8, below, 0)
        return carry

    lax.fori_loop(0, 8, step, 0)
    for j in range(4):
        v[j * 256 : j * 256 + 128, j * 256 + 128 : j * 256 + 256] = jnp.zeros((128, 128), F32)

    collect(1)
    swap_out(1).start()
    for c in gy:
        c.wait()
    gc.start()
    for w in range(2):
        swap_out(w).wait()
    for upper in range(2):
        for kr in range(6):
            for kc in range(6):
                norm_ref[pl.ds((2 * kr + upper) * 384 + kc, 64, stride=6), :] = out_ref[
                    upper, kr * 64 : kr * 64 + 64, kc * 64 : kc * 64 + 64]
    gc.wait()

    def panel(k, carry):
        for a in range(2):
            pieces = split(gt[a, pl.ds(k * 4, 4)].reshape(256, size))
            for u in range(12):
                q = (0, 1, 1, 0, 2, 0)[u // 2]
                yw[u // 3, (u % 3) * 128 : (u % 3) * 128 + 128, a * size : a * size + size] = (
                    pieces[q][(u % 2) * 128 : (u % 2) * 128 + 128])

        def one(j, carry):
            left = left_parts(v[pl.ds(pl.multiple_of(j * 256, 256), 256), pl.ds(pl.multiple_of(k * 256, 256), 256)])
            got = jnp.dot(left, yw[:, :, 0 : 2 * size].reshape(1536, 2 * size), preferred_element_type=F32)
            for a in range(2):
                for h in range(2):
                    at = j * 4 + a * 2 + h
                    new = got[h * 128 : h * 128 + 128, a * size : a * size + size]
                    dbuf[at, 0:128] = jnp.where(k == 0, new, dbuf[at, 0:128] + new)
            return carry

        lax.fori_loop(k, 4, one, 0)
        for a in range(2):
            for h in range(2):
                turned = dbuf[k * 4 + a * 2 + h, 0:128].T
                at = pl.ds(pl.multiple_of(k * 256 + h * 128, 128), 128)
                for upper in range(2):
                    for kc in range(3):
                        tile = 2 * (a * 3 + kc) + upper
                        panel_ref[tile * 64 : tile * 64 + 64, at] = turned[upper * half + kc * 64 : upper * half + kc * 64 + 64]
        return carry

    lax.fori_loop(0, 4, panel, 0)

    for c in range(len(CHUNKS)):
        zcopy(c, 0).wait_send()

        @pl.when(odd)
        def _():
            zcopy(c, 1).wait_send()

        for k in turns:
            ycopy(c, k).wait_send()
    for w in range(2):
        for b in range(12):
            final(b, w, "end")

        @pl.when(even)
        def _():
            for b in range(12, 20):
                final(b, w, "end")


def normal_and_panel(at, weight, prior):
    size, obs = at.shape
    dma = pltpu.SemaphoreType.DMA
    n = len(CHUNKS)
    return pl.pallas_call(
        kernel,
        out_shape=(jax.ShapeDtypeStruct((12 * size, 64), F32), jax.ShapeDtypeStruct((2 * size, 1024), F32)),
        in_specs=[VMEM] * 3,
        out_specs=(VMEM, VMEM),
        scratch_shapes=[
            pltpu.VMEM((2, size, size), F32),
            pltpu.VMEM((4, size, obs), BF16),
            pltpu.VMEM((2, size, obs), BF16),
            pltpu.VMEM((4, size, obs), BF16),
            pltpu.VMEM((2, size, obs), BF16),
            pltpu.VMEM((20, size, size), F32),
            pltpu.VMEM((20, size // 2, size), F32),
            pltpu.VMEM((20, size // 2, size - 128), BF16),
            pltpu.VMEM((3, 20, size // 8, 128), F32),
            pltpu.VMEM((3, 20, size // 8, size - 128), BF16),
            pltpu.VMEM((2, 2, 4, size // 8, size), F32),
            pltpu.VMEM((3, 64, 256), F32),
            pltpu.VMEM((3, 32, 256), F32),
            pltpu.VMEM((3, 32, 256), F32),
            pltpu.VMEM((4, 3, 8, 256), F32),
            pltpu.VMEM((2, 3, 8, 256), F32),
            pltpu.VMEM((2, 4, 4, 3, 32, 256), F32),
            pltpu.VMEM((1024, 1024), F32),
            pltpu.VMEM((768, 1024), BF16),
            pltpu.VMEM((2, 16, 64, size), F32),
            dma((n, 4)), dma((n, 4)), dma((n, 2)), dma((n, 2)), dma((3,)), dma((3,)),
            dma((4, 3)), dma((4, 3)), dma((4, 3)), dma((4, 3)), dma((2, 20)), dma((2, 2, 2, 4)), dma((2,)), dma((2,)),
            dma, dma, dma((4,)), dma((4,)), dma, dma, dma((4,)), dma((4,)), dma((2, 4)), dma((2, 4)), dma((2, 4)), dma((2, 4)), dma, dma,
            dma((4,)), dma((4,)), dma((4,)), dma((4,)), dma, dma,
        ],
        compiler_params=pltpu.CompilerParams(collective_id=0, has_side_effects=True, vmem_limit_bytes=60 << 20),
        name="normal_and_panel",
    )(at, weight, prior)


def body(design, obs_weight, prior):
    rows_dev, kc_tiles, single, tile = design.shape
    local_cols = kc_tiles * tile
    normal, panel = normal_and_panel(
        design.transpose(1, 2, 3, 0).reshape(local_cols, rows_dev), obs_weight.reshape(1, rows_dev), prior)
    shape = (2 * kc_tiles, 1, tile, kc_tiles, 1, tile)
    return (normal.reshape(shape), panel.reshape(2 * kc_tiles, 1, tile, 1024))


def solution(mesh):
    placed = (P(("arc", "row"), None, "col", None), P(("arc", "row")), P(None, "col", None))
    return jax.shard_map(
        body,
        mesh=mesh,
        in_specs=placed,
        out_specs=(P(None, "row", None, None, "col", None), P(None, "row", None, None)),
        check_vma=False,
    )
```

```python
import functools

import jax
import jax.numpy as jnp
from jax import lax
from jax.experimental import pallas as pl
from jax.experimental.pallas import tpu as pltpu
from jax.sharding import PartitionSpec as P

F32 = jnp.float32
BF16 = jnp.bfloat16
MESH = pl.DeviceIdType.MESH
VMEM = pl.BlockSpec(memory_space=pltpu.VMEM)
HIGHEST = lax.Precision.HIGHEST


def place():
    arc = lax.axis_index("arc")
    row = lax.axis_index("row")
    col = lax.axis_index("col")
    return arc, row // 2, row % 2, col // 4, col % 4


def device(arc, x, zh, y, zl):
    return (arc, x * 2 + zh, y * 4 + zl)


def pick(values, at):
    out = jnp.int32(values[0])
    for k in range(1, len(values)):
        out = jnp.where(at == k, values[k], out)
    return out


def factor_inverse(block):
    n = block.shape[0]
    lane = lax.broadcasted_iota(jnp.int32, (8, n), 1)
    sub = lax.broadcasted_iota(jnp.int32, (8, n), 0)
    groups = [block[8 * g : 8 * g + 8, :] for g in range(n // 8)]
    for q in range(n // 8):
        pivot = groups[q]
        inside = (lane >= 8 * q) & (lane < 8 * q + 8)
        cols = [jnp.broadcast_to(pivot[:, 8 * q + j : 8 * q + j + 1], (8, n)) for j in range(8)]
        rows = jnp.where(inside, (lane - 8 * q == sub).astype(F32), pivot)
        scale, mult, scaled = [], {}, []
        for j in range(8):
            r = lax.rsqrt(cols[j][j : j + 1, :])
            scale.append(r)
            m = jnp.where(sub > j, cols[j] * r, 0.0)
            for l in range(j + 1, 8):
                mult[j, l] = cols[l][j : j + 1, :] * r
                cols[l] = cols[l] - m * mult[j, l]
            top = rows[j : j + 1, :] * r
            scaled.append(top)
            rows = jnp.where(sub == j, top, rows - m * top)
        groups[q] = rows
        for g in range(q + 1, n // 8):
            low = groups[g]
            c = [jnp.broadcast_to(low[:, 8 * q + j : 8 * q + j + 1], (8, n)) for j in range(8)]
            low = jnp.where(inside, 0.0, low)
            for j in range(8):
                m = c[j] * scale[j]
                for l in range(j + 1, 8):
                    c[l] = c[l] - m * mult[j, l]
                low = low - m * scaled[j]
            groups[g] = low
    lane_all = lax.broadcasted_iota(jnp.int32, (n, n), 1)
    sub_all = lax.broadcasted_iota(jnp.int32, (n, n), 0)
    return jnp.where(lane_all <= sub_all, jnp.concatenate(groups, axis=0), 0.0)


CHUNKS = ((0, 64), (64, 128), (192, 192))
GROUPS = ((0, 9), (9, 3), (12, 8))


def kernel(at_ref, w_ref, prior_ref, norm_ref, panel_ref, out_ref,
           ya, za, yw, zw, part, dbuf, narrow, xf, xb, fbuf, strip, sbuf, mine, sx, sz, seen, v, rcat, gt,
           ysend, yrecv, zsend, zrecv, dsend, drecv, fxs, fxr, bxs, bxr, fsend, frecv, osend, orecv,
           s1s, s1r, s2s, s2r, s3s, s3r, s4s, s4r, s5s, s5r, s6s, s6r, s7s, s7r, gzs, gzr, gys, gyr, gcs, gcr):
    arc, x, zh, y, zl = place()
    size, obs = at_ref.shape
    half, piece = size // 2, size // 8
    even = zl % 2 == 0
    odd = jnp.logical_not(even)
    moved = (pick((1, 3, 0, 2), zl), pick((3, 0, 1, 0), zl))
    goes = (pick((2, 0, 3, 1), zl), pick((0, 2, 0, 0), zl))
    mate = device(1 - arc, x, zh, y, zl)
    zpeer = device(arc, x, 1 - zh, y, zl)
    col, row = y * 4 + zl, x * 2 + zh
    turns = (1, 3, 2)

    def xpeer(k):
        return device(arc, (x + k) % 4, zh, y, zl)

    def ypeer(k):
        return device(arc, x, zh, (y + k) % 4, zl)

    def lpeer(k):
        return device(arc, x, zh, y, (zl + k) % 4)

    def back(at, k):
        return (at + 4 - k) % 4

    def remote(src, dst, send, recv, target):
        return pltpu.make_async_remote_copy(src, dst, send, recv, device_id=target, device_id_type=MESH)

    blocks = [(kind, 0, k) for kind in ("own", "rows", "cols") for k in (0, 1, 3)]
    blocks += [(kind, 0, 2) for kind in ("own", "rows", "cols")]
    blocks += [(kind, 1, k) for kind in ("rows", "cols") for k in range(4)]

    def owner(block):
        kind, slot, k = block
        k = (y + k) % 4
        if kind == "own":
            y1, z1, y2, z2 = y, zl, k, zl
        elif kind == "rows":
            y1, z1, y2, z2 = y, moved[slot], k, zl
        else:
            y1, z1, y2, z2 = k, zl, y, moved[slot]
        r = (y1 % 2) * 4 + z1
        here = (r == row) & (y2 == y) & (z2 == zl)
        return (arc, r, y2 * 4 + z2), y1 // 2, here

    bar = pltpu.get_barrier_semaphore()

    def greet(target):
        pl.semaphore_signal(bar, inc=1, device_id=target, device_id_type=MESH)

    for k in turns:
        greet(ypeer(k))
        greet(xpeer(k))
        greet(lpeer(k))
    greet(mate)
    greet(zpeer)
    pl.semaphore_wait(bar, 11)

    def ycopy(c, k):
        at = pl.ds(*CHUNKS[c])
        return remote(at_ref.at[at], ya.at[y, at], ysend.at[c, k], yrecv.at[c, k], ypeer(k))

    def yarrival(c, k):
        at = pl.ds(*CHUNKS[c])
        return remote(at_ref.at[at], ya.at[back(y, k), at], ysend.at[c, k], yrecv.at[c, k], ypeer(k))

    def zcopy(c, s):
        at = pl.ds(*CHUNKS[c])
        return remote(at_ref.at[at], za.at[s, at], zsend.at[c, s], zrecv.at[c, s], device(arc, x, zh, y, goes[s]))

    def send_z(c, s):
        if s == 0:
            zcopy(c, 0).start()
        else:
            @pl.when(odd)
            def _():
                zcopy(c, 1).start()

    def send_y(c, ks):
        for k in ks:
            ycopy(c, k).start()

    def weigh(src, dst, c):
        first, rows = CHUNKS[c]

        def chunk(i, carry):
            at = pl.ds(pl.multiple_of(first + i * 32, 32), 32)
            dst[at, :] = (src[at, :].astype(F32) * w_ref[...]).astype(BF16)
            return carry

        lax.fori_loop(0, rows // 32, chunk, 0)

    def take_z(c, s):
        def go():
            zcopy(c, s).wait_recv()
            weigh(za.at[s], zw.at[s], c)

        if s == 0:
            go()
        else:
            pl.when(even)(go)

    def take_y(c, ks):
        for k in ks:
            yarrival(c, k).wait_recv()
            weigh(ya.at[back(y, k)], yw.at[back(y, k)], c)

    near, far = (1, 3), (2,)
    send_z(0, 0)
    send_y(0, near)
    send_z(0, 1)
    send_y(0, far)
    ya[y] = at_ref[...]
    for c in range(len(CHUNKS)):
        weigh(at_ref, yw.at[y], c)

    def nt(a, b):
        return lax.dot_general(a, b, (((1,), (1,)), ((), ())), preferred_element_type=F32)

    take_z(0, 0)
    take_y(0, near)
    take_z(0, 1)
    take_y(0, far)
    send_z(1, 0)
    send_y(1, near)
    ahead_w = yw[:, 0:64, :].reshape(256, obs)
    strip[0] = 0.5 * nt(at_ref[0:64, :], ahead_w)
    ahead_a = ya[:, 0:64, :].reshape(256, obs)
    strip[1] = 0.5 * (nt(za[0, 0:64, :], ahead_w) + nt(zw[0, 0:64, :], ahead_a))

    @pl.when(even)
    def _():
        strip[2] = 0.5 * (nt(za[1, 0:64, :], yw[:, 0:64, :].reshape(256, obs)) + nt(zw[1, 0:64, :], ya[:, 0:64, :].reshape(256, obs)))

    @pl.when(odd)
    def _():
        strip[2] = jnp.zeros((64, 256), F32)

    theirs = pl.ds(pl.multiple_of((1 - arc) * 32, 32), 32)
    ours = pl.ds(pl.multiple_of(arc * 32, 32), 32)
    s1 = remote(strip.at[:, theirs], sbuf, s1s, s1r, mate)
    s1.start()
    s1.wait()
    mine[...] = strip[:, ours] + sbuf[...]
    def share(k):
        return pl.ds(pl.multiple_of(((x + k) % 4) * 8, 8), 8)

    own = share(0)
    s2 = [remote(mine.at[:, share(k)], sx.at[x], s2s.at[k], s2r.at[k], xpeer(k)) for k in turns]
    for c in s2:
        c.start()
    sx[x] = mine[:, own]
    for c in s2:
        c.wait()
    sz[zh] = (sx[0] + sx[1]) + (sx[2] + sx[3])
    send_y(2, near)
    s3 = remote(sz.at[zh], sz.at[zh], s3s, s3r, zpeer)
    s3.start()
    s3.wait()
    sums = sz[0] + sz[1]
    lane = lax.broadcasted_iota(jnp.int32, (8, 256), 1)
    sub = lax.broadcasted_iota(jnp.int32, (8, 256), 0)
    prior4 = jnp.concatenate([prior_ref[0]] * 4, axis=1)
    diagonal = jnp.where(lane == y * 64 + arc * 32 + x * 8 + sub, 0.5 * prior4, 0.0)
    seen[arc, y, zl, 0, own] = sums[0] + diagonal
    seen[arc, y, zl, 1, own] = sums[1]
    seen[arc, y, zl, 2, own] = sums[2]
    view = seen.at[arc, y, zl, :, own]
    s4 = [remote(view, view, s4s.at[k], s4r.at[k], lpeer(k)) for k in turns]
    for c in s4:
        c.start()
    for c in s4:
        c.wait()
    low, high = pl.ds(0, 2), pl.ds(2, 2)

    def both_ways(first, second, send, recv):
        return ([remote(first, first, send.at[0, k], recv.at[0, k], xpeer(k)) for k in turns]
                + [remote(second, second, send.at[1, k], recv.at[1, k], ypeer(k)) for k in turns])

    s5 = both_ways(seen.at[arc, y, low, :, own], seen.at[arc, y, high, :, own], s5s, s5r)
    for c in s5:
        c.start()
    send_z(2, 0)
    for c in s5:
        c.wait()
    s6 = both_ways(seen.at[arc, :, high, :, own], seen.at[arc, y, low], s6s, s6r)
    for c in s6:
        c.start()
    send_z(1, 1)
    send_z(2, 1)
    send_y(1, far)
    send_y(2, far)
    s7 = remote(seen.at[arc], seen.at[arc], s7s, s7r, mate)

    def trade(g):
        first, n = GROUPS[g]
        return remote(part.at[pl.ds(first, n), pl.ds(pl.multiple_of((1 - arc) * half, half), half)],
                      dbuf.at[pl.ds(first, n)], dsend.at[g], drecv.at[g], mate)

    def products(first, n, kind, slot, shift):
        def one(i, carry):
            k = (y + shift(i)) % 4
            if kind == "own":
                part[first + i] = nt(at_ref[...], yw[k])
            elif kind == "rows":
                part[first + i] = nt(za[slot], yw[k])
            else:
                part[first + i] = nt(ya[k], zw[slot])
            return carry

        lax.fori_loop(0, n, one, 0)

    def first_products():
        for c in (1, 2):
            take_y(c, near)
            take_z(c, 0)
        for i, kind in enumerate(("own", "rows", "cols")):
            products(3 * i, 3, kind, 0, lambda i: i + jnp.where(i == 2, 1, 0))
        trade(0).start()

    def last_products():
        for c in (1, 2):
            take_y(c, far)
            take_z(c, 1)
        for i, kind in enumerate(("own", "rows", "cols")):
            products(9 + i, 1, kind, 0, lambda i: 2)
        trade(1).start()

        @pl.when(even)
        def _():
            products(12, 4, "rows", 1, lambda i: i)
            products(16, 4, "cols", 1, lambda i: i)
            trade(2).start()

    def fspread(g, k):
        first, n = GROUPS[g]
        at = pl.ds(pl.multiple_of(arc * half + ((x + k) % 4) * piece, 16), piece)
        return remote(part.at[pl.ds(first, n), at, pl.ds(0, 128)], xf.at[k - 1, pl.ds(first, n)],
                      fxs.at[k, g], fxr.at[k, g], xpeer(k))

    def bspread(g, k):
        first, n = GROUPS[g]
        at = pl.ds(pl.multiple_of(((x + k) % 4) * piece, 16), piece)
        return remote(narrow.at[pl.ds(first, n), at], xb.at[k - 1, pl.ds(first, n)],
                      bxs.at[k, g], bxr.at[k, g], xpeer(k))

    def halves(g):
        first, n = GROUPS[g]
        trade(g).wait()
        rows = pl.ds(pl.multiple_of(arc * half, half), half)

        def add(b, carry):
            both = part[first + b, rows] + dbuf[first + b]
            part[first + b, rows] = both
            narrow[first + b] = both[:, 128:].astype(BF16)
            return carry

        lax.fori_loop(0, n, add, 0)
        for k in turns:
            fspread(g, k).start()

    def spread_rest(g):
        for k in turns:
            bspread(g, k).start()

    lanes = (pl.ds(0, 128), pl.ds(128, size - 128))

    def final(b, w, act):
        target, upper, here = owner(blocks[b])
        src = part.at[b, pl.ds(pl.multiple_of(arc * half + x * piece, 16), piece), lanes[w]]
        dst = fbuf.at[upper, zh, x, :, lanes[w]]
        sem = frecv.at[w, upper, zh, x]

        @pl.when(here)
        def _():
            if act == "start":
                pltpu.make_async_copy(src, dst, sem).start()

        @pl.when(jnp.logical_not(here))
        def _():
            c = remote(src, dst, fsend.at[w, b], sem, target)
            if act == "start":
                c.start()
            else:
                c.wait_send()

    def deliver(g, w):
        first, n = GROUPS[g]
        rows = pl.ds(pl.multiple_of(arc * half + x * piece, 16), piece)
        spread, landed = (fspread, xf) if w == 0 else (bspread, xb)
        for k in turns:
            spread(g, k).wait()

        def add(b, carry):
            at = first + b
            part[at, rows, lanes[w]] = ((part[at, rows, lanes[w]] + landed[0, at].astype(F32))
                                      + (landed[1, at].astype(F32) + landed[2, at].astype(F32)))
            return carry

        lax.fori_loop(0, n, add, 0)
        for b in range(first, first + n):
            final(b, w, "start")

    def both(f, *rest):
        f(1, *rest)

        @pl.when(even)
        def _():
            f(2, *rest)

    prior_row = jnp.concatenate([prior_ref[k] for k in range(6)], axis=1)

    def collect(w):
        width = lanes[w].size
        lane = lax.broadcasted_iota(jnp.int32, (piece, width), 1) + lanes[w].start
        sub = lax.broadcasted_iota(jnp.int32, (piece, width), 0)
        for upper in range(2):
            for xx in range(4):
                for zz in range(2):
                    pltpu.make_async_copy(part.at[0, pl.ds(0, piece), lanes[w]], fbuf.at[upper, zz, xx, :, lanes[w]],
                                          frecv.at[w, upper, zz, xx]).wait()
                first = arc * half + xx * piece
                at = pl.ds(pl.multiple_of(first, 16), piece)
                hit = (lane == sub + first) & (col == row + 8 * upper)
                out_ref[upper, at, lanes[w]] = ((fbuf[upper, 0, xx, :, lanes[w]] + fbuf[upper, 1, xx, :, lanes[w]])
                                                + jnp.where(hit, prior_row[:, lanes[w].start : lanes[w].start + width], 0.0))

    def swap_out(w):
        view = out_ref.at[:, pl.ds(pl.multiple_of(arc * half, half), half), lanes[w]]
        return remote(view, view, osend.at[w], orecv.at[w], mate)

    most, others = pl.ds(0, 40), pl.ds(40, 24)
    here = (gt.at[arc, y, zl, most], gt.at[arc, y, zl, others])
    gz = ([remote(here[0], here[0], gzs.at[0, k], gzr.at[0, k], lpeer(k)) for k in turns]
          + [remote(here[1], here[1], gzs.at[1, k], gzr.at[1, k], ypeer(k)) for k in turns])
    there = (gt.at[arc, y, :, most], gt.at[arc, :, zl, others])
    gy = ([remote(there[0], there[0], gys.at[0, k], gyr.at[0, k], ypeer(k)) for k in turns]
          + [remote(there[1], there[1], gys.at[1, k], gyr.at[1, k], lpeer(k)) for k in turns])
    gc = remote(gt.at[arc], gt.at[arc], gcs, gcr, mate)

    first_products()
    for c in s6:
        c.wait()
    s7.start()
    halves(0)
    spread_rest(0)
    s7.wait()
    hosts = {0: (0, 1, 3), 1: (1, 3), 2: (2, 0, 1), 3: (3, 2)}

    def assemble(t, carry):
        a, yy = t // 4, t % 4
        for z1 in range(4):
            at = pl.ds(pl.multiple_of(yy * 256 + z1 * 64 + a * 32, 32), 32)
            for pair in range(2):
                sides = []
                for z2 in (2 * pair, 2 * pair + 1):
                    sides.append(seen[a, yy, z2, hosts[z2].index(z1)] if z1 in hosts[z2] else jnp.zeros((32, 256), F32))
                for y2 in range(4):
                    cut = slice(y2 * 64, y2 * 64 + 64)
                    v[at, y2 * 256 + pair * 128 : y2 * 256 + pair * 128 + 128] = jnp.concatenate(
                        [sides[0][:, cut], sides[1][:, cut]], axis=1)
        return carry

    lax.fori_loop(0, 8, assemble, 0)

    def symmetric(i, carry):
        at = pl.ds(pl.multiple_of(i * 128, 128), 128)

        def one(j, carry):
            here = pl.ds(pl.multiple_of(j * 128, 128), 128)
            whole = v[at, here] + v[here, at].T
            v[at, here] = whole
            v[here, at] = whole.T
            return carry

        return lax.fori_loop(i, 8, one, carry)

    lax.fori_loop(0, 8, symmetric, 0)

    def split(m):
        first = m.astype(BF16)
        rest = m - first.astype(F32)
        second = rest.astype(BF16)
        return first, second, (rest - second.astype(F32)).astype(BF16)

    def left_parts(m):
        a, b, c = split(m)
        return jnp.concatenate([a, b, a, b, a, c], axis=1)

    def right_parts(m):
        a, b, c = split(m)
        for i, q in enumerate((a, b, b, a, c, a)):
            rcat[i * 128 : i * 128 + 128, :] = q

    def step(p, carry):
        @pl.when(p == 1)
        def _():
            deliver(0, 0)
            last_products()

        @pl.when(p == 2)
        def _():
            both(deliver, 0)
            both(spread_rest)
            deliver(0, 1)

        @pl.when(p == 3)
        def _():
            collect(0)
            rows = pl.ds(pl.multiple_of(arc * half, half), half)
            for upper in range(2):
                gt[arc, y, zl, :, upper * half : upper * half + half] = out_ref[upper, rows, 0:128].T[0:64, :]
            for c in gz:
                c.start()
            swap_out(0).start()

        @pl.when(p == 4)
        def _():
            for c in gz:
                c.wait()
            for c in gy:
                c.start()
            both(deliver, 1)

        b = 128
        at = pl.ds(pl.multiple_of(p * b, b), b)
        inv = factor_inverse(v[at, at])

        @pl.when(p == 1)
        def _():
            both(halves)

        v[at, at] = jnp.eye(b, dtype=F32)
        right_parts(v[at, :])
        whole = jnp.dot(left_parts(inv), rcat[...], preferred_element_type=F32)
        v[at, :] = whole
        right_parts(whole)

        def below(i, carry):
            here = pl.ds(pl.multiple_of(i * b, b), b)
            left = left_parts(v[at, here].T)
            v[here, at] = jnp.zeros((b, b), F32)
            v[here, :] = v[here, :] - jnp.dot(left, rcat[...], preferred_element_type=F32)
            return carry

        lax.fori_loop(p + 1, 8, below, 0)
        return carry

    lax.fori_loop(0, 8, step, 0)
    for j in range(4):
        v[j * 256 : j * 256 + 128, j * 256 + 128 : j * 256 + 256] = jnp.zeros((128, 128), F32)

    collect(1)
    swap_out(1).start()
    for c in gy:
        c.wait()
    gc.start()
    for w in range(2):
        swap_out(w).wait()
    for upper in range(2):
        for kr in range(6):
            for kc in range(6):
                norm_ref[pl.ds((2 * kr + upper) * 384 + kc, 64, stride=6), :] = out_ref[
                    upper, kr * 64 : kr * 64 + 64, kc * 64 : kc * 64 + 64]
    gc.wait()

    def panel(k, carry):
        for a in range(2):
            pieces = split(gt[a, k].reshape(256, size))
            for u in range(12):
                q = (0, 1, 1, 0, 2, 0)[u // 2]
                yw[u // 3, (u % 3) * 128 : (u % 3) * 128 + 128, a * size : a * size + size] = (
                    pieces[q][(u % 2) * 128 : (u % 2) * 128 + 128])

        def one(j, carry):
            left = left_parts(v[pl.ds(pl.multiple_of(j * 256, 256), 256), pl.ds(pl.multiple_of(k * 256, 256), 256)])
            got = jnp.dot(left, yw[:, :, 0 : 2 * size].reshape(1536, 2 * size), preferred_element_type=F32)
            for a in range(2):
                for h in range(2):
                    at = j * 4 + a * 2 + h
                    new = got[h * 128 : h * 128 + 128, a * size : a * size + size]
                    dbuf[at, 0:128] = jnp.where(k == 0, new, dbuf[at, 0:128] + new)
            return carry

        lax.fori_loop(k, 4, one, 0)
        for a in range(2):
            for h in range(2):
                turned = dbuf[k * 4 + a * 2 + h, 0:128].T
                at = pl.ds(pl.multiple_of(k * 256 + h * 128, 128), 128)
                for upper in range(2):
                    for kc in range(3):
                        tile = 2 * (a * 3 + kc) + upper
                        panel_ref[tile * 64 : tile * 64 + 64, at] = turned[upper * half + kc * 64 : upper * half + kc * 64 + 64]
        return carry

    lax.fori_loop(0, 4, panel, 0)

    for c in range(len(CHUNKS)):
        zcopy(c, 0).wait_send()

        @pl.when(odd)
        def _():
            zcopy(c, 1).wait_send()

        for k in turns:
            ycopy(c, k).wait_send()
    for w in range(2):
        for b in range(12):
            final(b, w, "end")

        @pl.when(even)
        def _():
            for b in range(12, 20):
                final(b, w, "end")


def normal_and_panel(at, weight, prior):
    size, obs = at.shape
    dma = pltpu.SemaphoreType.DMA
    n = len(CHUNKS)
    return pl.pallas_call(
        kernel,
        out_shape=(jax.ShapeDtypeStruct((12 * size, 64), F32), jax.ShapeDtypeStruct((2 * size, 1024), F32)),
        in_specs=[VMEM] * 3,
        out_specs=(VMEM, VMEM),
        scratch_shapes=[
            pltpu.VMEM((2, size, size), F32),
            pltpu.VMEM((4, size, obs), BF16),
            pltpu.VMEM((2, size, obs), BF16),
            pltpu.VMEM((4, size, obs), BF16),
            pltpu.VMEM((2, size, obs), BF16),
            pltpu.VMEM((20, size, size), F32),
            pltpu.VMEM((20, size // 2, size), F32),
            pltpu.VMEM((20, size // 2, size - 128), BF16),
            pltpu.VMEM((3, 20, size // 8, 128), F32),
            pltpu.VMEM((3, 20, size // 8, size - 128), BF16),
            pltpu.VMEM((2, 2, 4, size // 8, size), F32),
            pltpu.VMEM((3, 64, 256), F32),
            pltpu.VMEM((3, 32, 256), F32),
            pltpu.VMEM((3, 32, 256), F32),
            pltpu.VMEM((4, 3, 8, 256), F32),
            pltpu.VMEM((2, 3, 8, 256), F32),
            pltpu.VMEM((2, 4, 4, 3, 32, 256), F32),
            pltpu.VMEM((1024, 1024), F32),
            pltpu.VMEM((768, 1024), BF16),
            pltpu.VMEM((2, 4, 4, 64, size), F32),
            dma((n, 4)), dma((n, 4)), dma((n, 2)), dma((n, 2)), dma((3,)), dma((3,)),
            dma((4, 3)), dma((4, 3)), dma((4, 3)), dma((4, 3)), dma((2, 20)), dma((2, 2, 2, 4)), dma((2,)), dma((2,)),
            dma, dma, dma((4,)), dma((4,)), dma, dma, dma((4,)), dma((4,)), dma((2, 4)), dma((2, 4)), dma((2, 4)), dma((2, 4)), dma, dma,
            dma((2, 4)), dma((2, 4)), dma((2, 4)), dma((2, 4)), dma, dma,
        ],
        compiler_params=pltpu.CompilerParams(collective_id=0, has_side_effects=True, vmem_limit_bytes=60 << 20),
        name="normal_and_panel",
    )(at, weight, prior)


def body(design, obs_weight, prior):
    rows_dev, kc_tiles, single, tile = design.shape
    local_cols = kc_tiles * tile
    normal, panel = normal_and_panel(
        design.transpose(1, 2, 3, 0).reshape(local_cols, rows_dev), obs_weight.reshape(1, rows_dev), prior)
    shape = (2 * kc_tiles, 1, tile, kc_tiles, 1, tile)
    return (normal.reshape(shape), panel.reshape(2 * kc_tiles, 1, tile, 1024))


def solution(mesh):
    placed = (P(("arc", "row"), None, "col", None), P(("arc", "row")), P(None, "col", None))
    return jax.shard_map(
        body,
        mesh=mesh,
        in_specs=placed,
        out_specs=(P(None, "row", None, None, "col", None), P(None, "row", None, None)),
        check_vma=False,
    )
```

```python
import functools

import jax
import jax.numpy as jnp
from jax import lax
from jax.experimental import pallas as pl
from jax.experimental.pallas import tpu as pltpu
from jax.sharding import PartitionSpec as P

F32 = jnp.float32
BF16 = jnp.bfloat16
MESH = pl.DeviceIdType.MESH
VMEM = pl.BlockSpec(memory_space=pltpu.VMEM)
HIGHEST = lax.Precision.HIGHEST


def place():
    arc = lax.axis_index("arc")
    row = lax.axis_index("row")
    col = lax.axis_index("col")
    return arc, row // 2, row % 2, col // 4, col % 4


def device(arc, x, zh, y, zl):
    return (arc, x * 2 + zh, y * 4 + zl)


def pick(values, at):
    out = jnp.int32(values[0])
    for k in range(1, len(values)):
        out = jnp.where(at == k, values[k], out)
    return out


def factor_inverse(block):
    n = block.shape[0]
    lane = lax.broadcasted_iota(jnp.int32, (8, n), 1)
    sub = lax.broadcasted_iota(jnp.int32, (8, n), 0)
    groups = [block[8 * g : 8 * g + 8, :] for g in range(n // 8)]
    for q in range(n // 8):
        pivot = groups[q]
        inside = (lane >= 8 * q) & (lane < 8 * q + 8)
        cols = [jnp.broadcast_to(pivot[:, 8 * q + j : 8 * q + j + 1], (8, n)) for j in range(8)]
        rows = jnp.where(inside, (lane - 8 * q == sub).astype(F32), pivot)
        scale, mult, scaled = [], {}, []
        for j in range(8):
            r = lax.rsqrt(cols[j][j : j + 1, :])
            scale.append(r)
            m = jnp.where(sub > j, cols[j] * r, 0.0)
            for l in range(j + 1, 8):
                mult[j, l] = cols[l][j : j + 1, :] * r
                cols[l] = cols[l] - m * mult[j, l]
            top = rows[j : j + 1, :] * r
            scaled.append(top)
            rows = jnp.where(sub == j, top, rows - m * top)
        groups[q] = rows
        for g in range(q + 1, n // 8):
            low = groups[g]
            c = [jnp.broadcast_to(low[:, 8 * q + j : 8 * q + j + 1], (8, n)) for j in range(8)]
            low = jnp.where(inside, 0.0, low)
            for j in range(8):
                m = c[j] * scale[j]
                for l in range(j + 1, 8):
                    c[l] = c[l] - m * mult[j, l]
                low = low - m * scaled[j]
            groups[g] = low
    lane_all = lax.broadcasted_iota(jnp.int32, (n, n), 1)
    sub_all = lax.broadcasted_iota(jnp.int32, (n, n), 0)
    return jnp.where(lane_all <= sub_all, jnp.concatenate(groups, axis=0), 0.0)


CHUNKS = ((0, 64), (64, 128), (192, 192))
GROUPS = ((0, 9), (9, 3), (12, 8))


def kernel(at_ref, w_ref, prior_ref, norm_ref, panel_ref, out_ref,
           ya, za, yw, zw, part, dbuf, narrow, xf, xb, fbuf, strip, sbuf, mine, sx, sz, seen, v, rcat, gt,
           ysend, yrecv, zsend, zrecv, dsend, drecv, fxs, fxr, bxs, bxr, fsend, frecv, osend, orecv,
           s1s, s1r, s2s, s2r, s3s, s3r, s4s, s4r, s5s, s5r, s6s, s6r, s7s, s7r, gzs, gzr, gys, gyr, gcs, gcr):
    arc, x, zh, y, zl = place()
    size, obs = at_ref.shape
    half, piece = size // 2, size // 8
    even = zl % 2 == 0
    odd = jnp.logical_not(even)
    moved = (pick((1, 3, 0, 2), zl), pick((3, 0, 1, 0), zl))
    goes = (pick((2, 0, 3, 1), zl), pick((0, 2, 0, 0), zl))
    mate = device(1 - arc, x, zh, y, zl)
    zpeer = device(arc, x, 1 - zh, y, zl)
    col, row = y * 4 + zl, x * 2 + zh
    turns = (1, 3, 2)

    def xpeer(k):
        return device(arc, (x + k) % 4, zh, y, zl)

    def ypeer(k):
        return device(arc, x, zh, (y + k) % 4, zl)

    def lpeer(k):
        return device(arc, x, zh, y, (zl + k) % 4)

    def back(at, k):
        return (at + 4 - k) % 4

    def remote(src, dst, send, recv, target):
        return pltpu.make_async_remote_copy(src, dst, send, recv, device_id=target, device_id_type=MESH)

    blocks = [(kind, 0, k) for kind in ("own", "rows", "cols") for k in (0, 1, 3)]
    blocks += [(kind, 0, 2) for kind in ("own", "rows", "cols")]
    blocks += [(kind, 1, k) for kind in ("rows", "cols") for k in range(4)]

    def owner(block):
        kind, slot, k = block
        k = (y + k) % 4
        if kind == "own":
            y1, z1, y2, z2 = y, zl, k, zl
        elif kind == "rows":
            y1, z1, y2, z2 = y, moved[slot], k, zl
        else:
            y1, z1, y2, z2 = k, zl, y, moved[slot]
        r = (y1 % 2) * 4 + z1
        here = (r == row) & (y2 == y) & (z2 == zl)
        return (arc, r, y2 * 4 + z2), y1 // 2, here

    bar = pltpu.get_barrier_semaphore()

    def greet(target):
        pl.semaphore_signal(bar, inc=1, device_id=target, device_id_type=MESH)

    for k in turns:
        greet(ypeer(k))
        greet(xpeer(k))
        greet(lpeer(k))
    greet(mate)
    greet(zpeer)
    pl.semaphore_wait(bar, 11)

    def ycopy(c, k):
        at = pl.ds(*CHUNKS[c])
        return remote(at_ref.at[at], ya.at[y, at], ysend.at[c, k], yrecv.at[c, k], ypeer(k))

    def yarrival(c, k):
        at = pl.ds(*CHUNKS[c])
        return remote(at_ref.at[at], ya.at[back(y, k), at], ysend.at[c, k], yrecv.at[c, k], ypeer(k))

    def zcopy(c, s):
        at = pl.ds(*CHUNKS[c])
        return remote(at_ref.at[at], za.at[s, at], zsend.at[c, s], zrecv.at[c, s], device(arc, x, zh, y, goes[s]))

    def send_z(c, s):
        if s == 0:
            zcopy(c, 0).start()
        else:
            @pl.when(odd)
            def _():
                zcopy(c, 1).start()

    def send_y(c, ks):
        for k in ks:
            ycopy(c, k).start()

    def weigh(src, dst, c):
        first, rows = CHUNKS[c]

        def chunk(i, carry):
            at = pl.ds(pl.multiple_of(first + i * 32, 32), 32)
            dst[at, :] = (src[at, :].astype(F32) * w_ref[...]).astype(BF16)
            return carry

        lax.fori_loop(0, rows // 32, chunk, 0)

    def take_z(c, s):
        def go():
            zcopy(c, s).wait_recv()
            weigh(za.at[s], zw.at[s], c)

        if s == 0:
            go()
        else:
            pl.when(even)(go)

    def take_y(c, ks):
        for k in ks:
            yarrival(c, k).wait_recv()
            weigh(ya.at[back(y, k)], yw.at[back(y, k)], c)

    near, far = (1, 3), (2,)
    send_z(0, 0)
    send_y(0, near)
    send_z(0, 1)
    send_y(0, far)
    ya[y] = at_ref[...]
    for c in range(len(CHUNKS)):
        weigh(at_ref, yw.at[y], c)

    def nt(a, b):
        return lax.dot_general(a, b, (((1,), (1,)), ((), ())), preferred_element_type=F32)

    take_z(0, 0)
    take_y(0, near)
    take_z(0, 1)
    take_y(0, far)
    send_z(1, 0)
    send_y(1, near)
    ahead_w = yw[:, 0:64, :].reshape(256, obs)
    strip[0] = 0.5 * nt(at_ref[0:64, :], ahead_w)
    ahead_a = ya[:, 0:64, :].reshape(256, obs)
    strip[1] = 0.5 * (nt(za[0, 0:64, :], ahead_w) + nt(zw[0, 0:64, :], ahead_a))

    @pl.when(even)
    def _():
        strip[2] = 0.5 * (nt(za[1, 0:64, :], yw[:, 0:64, :].reshape(256, obs)) + nt(zw[1, 0:64, :], ya[:, 0:64, :].reshape(256, obs)))

    @pl.when(odd)
    def _():
        strip[2] = jnp.zeros((64, 256), F32)

    theirs = pl.ds(pl.multiple_of((1 - arc) * 32, 32), 32)
    ours = pl.ds(pl.multiple_of(arc * 32, 32), 32)
    s1 = remote(strip.at[:, theirs], sbuf, s1s, s1r, mate)
    s1.start()
    s1.wait()
    mine[...] = strip[:, ours] + sbuf[...]
    def share(k):
        return pl.ds(pl.multiple_of(((x + k) % 4) * 8, 8), 8)

    own = share(0)
    s2 = [remote(mine.at[:, share(k)], sx.at[x], s2s.at[k], s2r.at[k], xpeer(k)) for k in turns]
    for c in s2:
        c.start()
    sx[x] = mine[:, own]
    for c in s2:
        c.wait()
    sz[zh] = (sx[0] + sx[1]) + (sx[2] + sx[3])
    send_y(2, near)
    s3 = remote(sz.at[zh], sz.at[zh], s3s, s3r, zpeer)
    s3.start()
    s3.wait()
    sums = sz[0] + sz[1]
    lane = lax.broadcasted_iota(jnp.int32, (8, 256), 1)
    sub = lax.broadcasted_iota(jnp.int32, (8, 256), 0)
    prior4 = jnp.concatenate([prior_ref[0]] * 4, axis=1)
    diagonal = jnp.where(lane == y * 64 + arc * 32 + x * 8 + sub, 0.5 * prior4, 0.0)
    seen[arc, y, zl, 0, own] = sums[0] + diagonal
    seen[arc, y, zl, 1, own] = sums[1]
    seen[arc, y, zl, 2, own] = sums[2]
    view = seen.at[arc, y, zl, :, own]
    s4 = [remote(view, view, s4s.at[k], s4r.at[k], lpeer(k)) for k in turns]
    for c in s4:
        c.start()
    for c in s4:
        c.wait()
    low, high = pl.ds(0, 2), pl.ds(2, 2)

    def both_ways(first, second, send, recv):
        return ([remote(first, first, send.at[0, k], recv.at[0, k], xpeer(k)) for k in turns]
                + [remote(second, second, send.at[1, k], recv.at[1, k], ypeer(k)) for k in turns])

    s5 = both_ways(seen.at[arc, y, low, :, own], seen.at[arc, y, high, :, own], s5s, s5r)
    for c in s5:
        c.start()
    send_z(2, 0)
    for c in s5:
        c.wait()
    s6 = both_ways(seen.at[arc, :, high, :, own], seen.at[arc, y, low], s6s, s6r)
    for c in s6:
        c.start()
    send_z(1, 1)
    send_z(2, 1)
    send_y(1, far)
    send_y(2, far)
    s7 = remote(seen.at[arc], seen.at[arc], s7s, s7r, mate)

    def trade(g):
        first, n = GROUPS[g]
        return remote(part.at[pl.ds(first, n), pl.ds(pl.multiple_of((1 - arc) * half, half), half)],
                      dbuf.at[pl.ds(first, n)], dsend.at[g], drecv.at[g], mate)

    def products(first, n, kind, slot, shift):
        def one(i, carry):
            k = (y + shift(i)) % 4
            if kind == "own":
                part[first + i] = nt(at_ref[...], yw[k])
            elif kind == "rows":
                part[first + i] = nt(za[slot], yw[k])
            else:
                part[first + i] = nt(ya[k], zw[slot])
            return carry

        lax.fori_loop(0, n, one, 0)

    def first_products():
        for c in (1, 2):
            take_y(c, near)
            take_z(c, 0)
        for i, kind in enumerate(("own", "rows", "cols")):
            products(3 * i, 3, kind, 0, lambda i: i + jnp.where(i == 2, 1, 0))
        trade(0).start()

    def last_products():
        for c in (1, 2):
            take_y(c, far)
            take_z(c, 1)
        for i, kind in enumerate(("own", "rows", "cols")):
            products(9 + i, 1, kind, 0, lambda i: 2)
        trade(1).start()

        @pl.when(even)
        def _():
            products(12, 4, "rows", 1, lambda i: i)
            products(16, 4, "cols", 1, lambda i: i)
            trade(2).start()

    def fspread(g, k):
        first, n = GROUPS[g]
        at = pl.ds(pl.multiple_of(arc * half + ((x + k) % 4) * piece, 16), piece)
        return remote(part.at[pl.ds(first, n), at, pl.ds(0, 128)], xf.at[k - 1, pl.ds(first, n)],
                      fxs.at[k, g], fxr.at[k, g], xpeer(k))

    def bspread(g, k):
        first, n = GROUPS[g]
        at = pl.ds(pl.multiple_of(((x + k) % 4) * piece, 16), piece)
        return remote(narrow.at[pl.ds(first, n), at], xb.at[k - 1, pl.ds(first, n)],
                      bxs.at[k, g], bxr.at[k, g], xpeer(k))

    def halves(g):
        first, n = GROUPS[g]
        trade(g).wait()
        rows = pl.ds(pl.multiple_of(arc * half, half), half)

        def add(b, carry):
            both = part[first + b, rows] + dbuf[first + b]
            part[first + b, rows] = both
            narrow[first + b] = both[:, 128:].astype(BF16)
            return carry

        lax.fori_loop(0, n, add, 0)
        for k in turns:
            fspread(g, k).start()

    def spread_rest(g):
        for k in turns:
            bspread(g, k).start()

    lanes = (pl.ds(0, 128), pl.ds(128, size - 128))

    def final(b, w, act):
        target, upper, here = owner(blocks[b])
        src = part.at[b, pl.ds(pl.multiple_of(arc * half + x * piece, 16), piece), lanes[w]]
        dst = fbuf.at[upper, zh, x, :, lanes[w]]
        sem = frecv.at[w, upper, zh, x]

        @pl.when(here)
        def _():
            if act == "start":
                pltpu.make_async_copy(src, dst, sem).start()

        @pl.when(jnp.logical_not(here))
        def _():
            c = remote(src, dst, fsend.at[w, b], sem, target)
            if act == "start":
                c.start()
            else:
                c.wait_send()

    def deliver(g, w):
        first, n = GROUPS[g]
        rows = pl.ds(pl.multiple_of(arc * half + x * piece, 16), piece)
        spread, landed = (fspread, xf) if w == 0 else (bspread, xb)
        for k in turns:
            spread(g, k).wait()

        def add(b, carry):
            at = first + b
            part[at, rows, lanes[w]] = ((part[at, rows, lanes[w]] + landed[0, at].astype(F32))
                                      + (landed[1, at].astype(F32) + landed[2, at].astype(F32)))
            return carry

        lax.fori_loop(0, n, add, 0)
        for b in range(first, first + n):
            final(b, w, "start")

    def both(f, *rest):
        f(1, *rest)

        @pl.when(even)
        def _():
            f(2, *rest)

    prior_row = jnp.concatenate([prior_ref[k] for k in range(6)], axis=1)

    def collect(w):
        width = lanes[w].size
        lane = lax.broadcasted_iota(jnp.int32, (piece, width), 1) + lanes[w].start
        sub = lax.broadcasted_iota(jnp.int32, (piece, width), 0)
        for upper in range(2):
            for xx in range(4):
                for zz in range(2):
                    pltpu.make_async_copy(part.at[0, pl.ds(0, piece), lanes[w]], fbuf.at[upper, zz, xx, :, lanes[w]],
                                          frecv.at[w, upper, zz, xx]).wait()
                first = arc * half + xx * piece
                at = pl.ds(pl.multiple_of(first, 16), piece)
                hit = (lane == sub + first) & (col == row + 8 * upper)
                out_ref[upper, at, lanes[w]] = ((fbuf[upper, 0, xx, :, lanes[w]] + fbuf[upper, 1, xx, :, lanes[w]])
                                                + jnp.where(hit, prior_row[:, lanes[w].start : lanes[w].start + width], 0.0))

    def swap_out(w):
        view = out_ref.at[:, pl.ds(pl.multiple_of(arc * half, half), half), lanes[w]]
        return remote(view, view, osend.at[w], orecv.at[w], mate)

    most, others = pl.ds(0, 40), pl.ds(40, 24)
    here = (gt.at[arc, y, zl, most], gt.at[arc, y, zl, others])
    gz = ([remote(here[0], here[0], gzs.at[0, k], gzr.at[0, k], lpeer(k)) for k in turns]
          + [remote(here[1], here[1], gzs.at[1, k], gzr.at[1, k], ypeer(k)) for k in turns])
    there = (gt.at[arc, y, :, most], gt.at[arc, :, zl, others])
    gy = ([remote(there[0], there[0], gys.at[0, k], gyr.at[0, k], ypeer(k)) for k in turns]
          + [remote(there[1], there[1], gys.at[1, k], gyr.at[1, k], lpeer(k)) for k in turns])
    gc = remote(gt.at[arc], gt.at[arc], gcs, gcr, mate)

    first_products()
    for c in s6:
        c.wait()
    s7.start()
    halves(0)
    spread_rest(0)
    s7.wait()
    hosts = {0: (0, 1, 3), 1: (1, 3), 2: (2, 0, 1), 3: (3, 2)}

    def assemble(t, carry):
        a, yy = t // 4, t % 4
        for z1 in range(4):
            at = pl.ds(pl.multiple_of(yy * 256 + z1 * 64 + a * 32, 32), 32)
            for pair in range(2):
                sides = []
                for z2 in (2 * pair, 2 * pair + 1):
                    sides.append(seen[a, yy, z2, hosts[z2].index(z1)] if z1 in hosts[z2] else jnp.zeros((32, 256), F32))
                for y2 in range(4):
                    cut = slice(y2 * 64, y2 * 64 + 64)
                    v[at, y2 * 256 + pair * 128 : y2 * 256 + pair * 128 + 128] = jnp.concatenate(
                        [sides[0][:, cut], sides[1][:, cut]], axis=1)
        return carry

    lax.fori_loop(0, 8, assemble, 0)

    def symmetric(i, carry):
        at = pl.ds(pl.multiple_of(i * 128, 128), 128)

        def one(j, carry):
            here = pl.ds(pl.multiple_of(j * 128, 128), 128)
            whole = v[at, here] + v[here, at].T
            v[at, here] = whole
            v[here, at] = whole.T
            return carry

        return lax.fori_loop(i, 8, one, carry)

    lax.fori_loop(0, 8, symmetric, 0)

    def split(m):
        first = m.astype(BF16)
        rest = m - first.astype(F32)
        second = rest.astype(BF16)
        return first, second, (rest - second.astype(F32)).astype(BF16)

    def left_parts(m):
        a, b, c = split(m)
        return jnp.concatenate([a, b, a, b, a, c], axis=1)

    def right_parts(m):
        a, b, c = split(m)
        for i, q in enumerate((a, b, b, a, c, a)):
            rcat[i * 128 : i * 128 + 128, :] = q

    def step(p, carry):
        @pl.when(p == 1)
        def _():
            deliver(0, 0)
            last_products()

        @pl.when(p == 3)
        def _():
            collect(0)
            rows = pl.ds(pl.multiple_of(arc * half, half), half)
            for upper in range(2):
                gt[arc, y, zl, :, upper * half : upper * half + half] = out_ref[upper, rows, 0:128].T[0:64, :]
            for c in gz:
                c.start()
            swap_out(0).start()

        @pl.when(p == 4)
        def _():
            for c in gz:
                c.wait()
            for c in gy:
                c.start()
            both(deliver, 1)

        b = 128
        at = pl.ds(pl.multiple_of(p * b, b), b)
        inv = factor_inverse(v[at, at])

        @pl.when(p == 1)
        def _():
            both(halves)

        @pl.when(p == 2)
        def _():
            both(deliver, 0)
            both(spread_rest)
            deliver(0, 1)

        v[at, at] = jnp.eye(b, dtype=F32)
        right_parts(v[at, :])
        whole = jnp.dot(left_parts(inv), rcat[...], preferred_element_type=F32)
        v[at, :] = whole
        right_parts(whole)

        def below(i, carry):
            here = pl.ds(pl.multiple_of(i * b, b), b)
            left = left_parts(v[at, here].T)
            v[here, at] = jnp.zeros((b, b), F32)
            v[here, :] = v[here, :] - jnp.dot(left, rcat[...], preferred_element_type=F32)
            return carry

        lax.fori_loop(p + 1, 8, below, 0)
        return carry

    lax.fori_loop(0, 8, step, 0)
    for j in range(4):
        v[j * 256 : j * 256 + 128, j * 256 + 128 : j * 256 + 256] = jnp.zeros((128, 128), F32)

    collect(1)
    swap_out(1).start()
    for c in gy:
        c.wait()
    gc.start()
    for w in range(2):
        swap_out(w).wait()
    for upper in range(2):
        for kr in range(6):
            for kc in range(6):
                norm_ref[pl.ds((2 * kr + upper) * 384 + kc, 64, stride=6), :] = out_ref[
                    upper, kr * 64 : kr * 64 + 64, kc * 64 : kc * 64 + 64]
    gc.wait()

    def panel(k, carry):
        for a in range(2):
            pieces = split(gt[a, k].reshape(256, size))
            for u in range(12):
                q = (0, 1, 1, 0, 2, 0)[u // 2]
                yw[u // 3, (u % 3) * 128 : (u % 3) * 128 + 128, a * size : a * size + size] = (
                    pieces[q][(u % 2) * 128 : (u % 2) * 128 + 128])

        def one(j, carry):
            left = left_parts(v[pl.ds(pl.multiple_of(j * 256, 256), 256), pl.ds(pl.multiple_of(k * 256, 256), 256)])
            got = jnp.dot(left, yw[:, :, 0 : 2 * size].reshape(1536, 2 * size), preferred_element_type=F32)
            for a in range(2):
                for h in range(2):
                    at = j * 4 + a * 2 + h
                    new = got[h * 128 : h * 128 + 128, a * size : a * size + size]
                    dbuf[at, 0:128] = jnp.where(k == 0, new, dbuf[at, 0:128] + new)
            return carry

        lax.fori_loop(k, 4, one, 0)
        for a in range(2):
            for h in range(2):
                turned = dbuf[k * 4 + a * 2 + h, 0:128].T
                at = pl.ds(pl.multiple_of(k * 256 + h * 128, 128), 128)
                for upper in range(2):
                    for kc in range(3):
                        tile = 2 * (a * 3 + kc) + upper
                        panel_ref[tile * 64 : tile * 64 + 64, at] = turned[upper * half + kc * 64 : upper * half + kc * 64 + 64]
        return carry

    lax.fori_loop(0, 4, panel, 0)

    for c in range(len(CHUNKS)):
        zcopy(c, 0).wait_send()

        @pl.when(odd)
        def _():
            zcopy(c, 1).wait_send()

        for k in turns:
            ycopy(c, k).wait_send()
    for w in range(2):
        for b in range(12):
            final(b, w, "end")

        @pl.when(even)
        def _():
            for b in range(12, 20):
                final(b, w, "end")


def normal_and_panel(at, weight, prior):
    size, obs = at.shape
    dma = pltpu.SemaphoreType.DMA
    n = len(CHUNKS)
    return pl.pallas_call(
        kernel,
        out_shape=(jax.ShapeDtypeStruct((12 * size, 64), F32), jax.ShapeDtypeStruct((2 * size, 1024), F32)),
        in_specs=[VMEM] * 3,
        out_specs=(VMEM, VMEM),
        scratch_shapes=[
            pltpu.VMEM((2, size, size), F32),
            pltpu.VMEM((4, size, obs), BF16),
            pltpu.VMEM((2, size, obs), BF16),
            pltpu.VMEM((4, size, obs), BF16),
            pltpu.VMEM((2, size, obs), BF16),
            pltpu.VMEM((20, size, size), F32),
            pltpu.VMEM((20, size // 2, size), F32),
            pltpu.VMEM((20, size // 2, size - 128), BF16),
            pltpu.VMEM((3, 20, size // 8, 128), F32),
            pltpu.VMEM((3, 20, size // 8, size - 128), BF16),
            pltpu.VMEM((2, 2, 4, size // 8, size), F32),
            pltpu.VMEM((3, 64, 256), F32),
            pltpu.VMEM((3, 32, 256), F32),
            pltpu.VMEM((3, 32, 256), F32),
            pltpu.VMEM((4, 3, 8, 256), F32),
            pltpu.VMEM((2, 3, 8, 256), F32),
            pltpu.VMEM((2, 4, 4, 3, 32, 256), F32),
            pltpu.VMEM((1024, 1024), F32),
            pltpu.VMEM((768, 1024), BF16),
            pltpu.VMEM((2, 4, 4, 64, size), F32),
            dma((n, 4)), dma((n, 4)), dma((n, 2)), dma((n, 2)), dma((3,)), dma((3,)),
            dma((4, 3)), dma((4, 3)), dma((4, 3)), dma((4, 3)), dma((2, 20)), dma((2, 2, 2, 4)), dma((2,)), dma((2,)),
            dma, dma, dma((4,)), dma((4,)), dma, dma, dma((4,)), dma((4,)), dma((2, 4)), dma((2, 4)), dma((2, 4)), dma((2, 4)), dma, dma,
            dma((2, 4)), dma((2, 4)), dma((2, 4)), dma((2, 4)), dma, dma,
        ],
        compiler_params=pltpu.CompilerParams(collective_id=0, has_side_effects=True, vmem_limit_bytes=60 << 20),
        name="normal_and_panel",
    )(at, weight, prior)


def body(design, obs_weight, prior):
    rows_dev, kc_tiles, single, tile = design.shape
    local_cols = kc_tiles * tile
    normal, panel = normal_and_panel(
        design.transpose(1, 2, 3, 0).reshape(local_cols, rows_dev), obs_weight.reshape(1, rows_dev), prior)
    shape = (2 * kc_tiles, 1, tile, kc_tiles, 1, tile)
    return (normal.reshape(shape), panel.reshape(2 * kc_tiles, 1, tile, 1024))


def solution(mesh):
    placed = (P(("arc", "row"), None, "col", None), P(("arc", "row")), P(None, "col", None))
    return jax.shard_map(
        body,
        mesh=mesh,
        in_specs=placed,
        out_specs=(P(None, "row", None, None, "col", None), P(None, "row", None, None)),
        check_vma=False,
    )
```
